512 devices in a mesh: walk: 32 (over z, y_hi, core), pb: 16 (over y_lo, x).
Axes of the slice: x: 4, y: 8 (y_hi: 2, y_lo: 4; y = y_hi * 4 + y_lo), z: 8, core: 2. Of those that a mesh axis runs over, the one named last changes fastest.
Arguments:
- bras: bfloat16 [256, 4, 4, 208], P('walk'), may hold values from -6 to 6
- fields: float32 [1, 256, 4, 160], P(None, 'walk'), may hold values from -5 to 5
- chol: bfloat16 [16, 160, 21632], P('pb', 'walk'), may hold values from -0.0234375 to 0.0234375
- one_body: bfloat16 [4, 21632], replicated, may hold values from -0.4375 to 0.4375
- pair_table: int32 [16, 2], replicated, may hold values from 0 to 3, as said below
- kpq_map: int32 [4, 4], replicated, may hold values from 0 to 3, as said below
Outputs:
- new_bras: bfloat16 [256, 4, 4, 208], P('walk')
The draws below stay inside these ranges and needn't reach their ends.
Inputs may be any that keep to these rules, and one draw needn't show every extreme that they name: `pair_table`: each row holds a momentum transfer and a k-point; each of the 16 pairs stands in exactly one row. kpq_map[Q, k] is the sum k+Q of an abelian group on the 4 k-points; each row and each column is a permutation of the k-points.
All inputs are finite; a program needn't handle non-finite values.
Results may differ from the reference program's by a relative error of at most 0.009.
Values may be sent and summed in bfloat16 or wider, within the bound.
A program may use at most 64 MiB of HBM per device.

```python
import jax
import jax.numpy as jnp
from jax import lax

NORB = 104
NCHOL = 160
NOCC = 4
NK = 4
STEPS = 1
ORDER = 4
WALKERS = 256
NPAIRS = 16


def draw_pair_table(key, part):
    key = jax.random.fold_in(key, 11)
    shuffled = jax.random.permutation(key, NK * NK).astype(jnp.int32)
    return jnp.stack([shuffled // NK, shuffled % NK], axis=-1).astype(jnp.int32)


def draw_kpq_map(key, part):
    key = jax.random.fold_in(key, 23)
    labels = jax.random.permutation(key, NK).astype(jnp.int32)
    position = jnp.zeros((NK,), jnp.int32).at[labels].set(jnp.arange(NK, dtype=jnp.int32))
    summed = (position[:, None] + position[None, :]) % NK
    return labels[summed].astype(jnp.int32)


def levels(own_key, shape, pieces, least, largest):
    level, own = 1.0, jax.random.fold_in(own_key, 6)
    for dim, blocks in pieces:
        steps = jnp.exp(jax.random.uniform(jax.random.fold_in(own, dim), (blocks,), jnp.float32, least / len(pieces), largest / len(pieces)))
        level = level * jnp.repeat(steps, shape[dim] // blocks).reshape([-1 if axis == dim else 1 for axis in range(len(shape))])
    return level


def scatter_about(own_key, dims, scale, reach, pieces=(), kind=jnp.bfloat16):
    entries = jax.random.normal(own_key, dims, jnp.float32) * scale
    if len(pieces) > 0:
        entries = levels(own_key, dims, pieces, -0.22, 0.18) * entries
    return jnp.clip(entries, min=-reach, max=reach).astype(kind)


def setup_inputs(seed: int = 0) -> dict:
    key_list = jax.random.split(jax.random.key(seed), 7)
    bras = scatter_about(key_list[0], (WALKERS, NK, NOCC, 2 * NORB), 1.0, 6.0, ((0, 32),))
    fields = scatter_about(key_list[1], (STEPS, WALKERS, NK, NCHOL), 1.0, 5.0, ((1, 32),), jnp.float32)
    chol = scatter_about(key_list[2], (NPAIRS, NCHOL, 2 * NORB * NORB), (NCHOL * NORB * NK) ** -0.5, 0.0234375, ((0, 16), (1, 32)))
    one_body = scatter_about(key_list[3], (NK, 2 * NORB * NORB), (2 * NORB) ** -0.5, 0.4375)
    pair_table = draw_pair_table(jax.random.fold_in(key_list[6], 71), 0)
    kpq_map = draw_kpq_map(jax.random.fold_in(key_list[6], 71), 0)
    return {"bras": bras, "fields": fields, "chol": chol, "one_body": one_body, "pair_table": pair_table, "kpq_map": kpq_map}


def split_parts(source, orbitals):
    return source[..., :orbitals], source[..., orbitals:]


def complex_join(product, orbitals):
    real_part = product[0, ..., :orbitals] - product[1, ..., orbitals:]
    imag_part = product[0, ..., orbitals:] + product[1, ..., :orbitals]
    return jnp.concatenate([real_part, imag_part], axis=-1)


def propagate_one_body(sectioned, one_body):
    real_half, imag_half = split_parts(sectioned, NORB)
    matrix = one_body.astype(jnp.float32).reshape(NK, NORB, 2 * NORB)
    first_half = jnp.einsum("wkin,knd->wkid", real_half.astype(jnp.float32), matrix)
    second_half = jnp.einsum("wkin,knd->wkid", imag_half.astype(jnp.float32), matrix)
    return complex_join(jnp.stack([first_half, second_half], axis=0), NORB).astype(jnp.bfloat16)


def transfer_terms(current_term, field_step, chol, pair_table, kpq_map):
    walkers = current_term.shape[0]

    def add_pair(pair_index, by_target):
        charge = pair_table[pair_index, 0]
        kpoint = pair_table[pair_index, 1]
        target = kpq_map[charge, kpoint]
        source = lax.dynamic_index_in_dim(current_term, kpoint, axis=1, keepdims=False)
        field_row = lax.dynamic_index_in_dim(field_step, charge, axis=1, keepdims=False)
        halves = jnp.stack(split_parts(source, NORB), axis=0).astype(jnp.float32)
        weighted = (field_row[None, :, None, :, None] * halves[:, :, :, None, :]).astype(jnp.bfloat16)
        weighted = weighted.reshape(2 * walkers * NOCC, NCHOL * NORB)
        matrix = lax.dynamic_index_in_dim(chol, pair_index, axis=0, keepdims=False).reshape(NCHOL * NORB, 2 * NORB)
        product = jnp.dot(weighted, matrix, preferred_element_type=jnp.float32).reshape(2, walkers, NOCC, 2 * NORB)
        contrib = complex_join(product, NORB)
        current = lax.dynamic_index_in_dim(by_target, target, axis=1, keepdims=False)
        return lax.dynamic_update_index_in_dim(by_target, current + contrib, target, axis=1)

    by_target = jnp.zeros((walkers, NK, NOCC, 2 * NORB), jnp.float32)
    return lax.fori_loop(0, NK * NK, add_pair, by_target)


def reference(bras, fields, chol, one_body, pair_table, kpq_map):
    bra_state = bras
    for saved_step in reversed(range(STEPS)):
        field_step = fields[saved_step]
        current_term = bra_state
        summed_terms = bra_state.astype(jnp.float32)
        for taylor in range(1, ORDER + 1):
            scaled = transfer_terms(current_term, field_step, chol, pair_table, kpq_map) / float(taylor)
            summed_terms = summed_terms + scaled
            current_term = scaled.astype(jnp.bfloat16)
        sectioned = summed_terms.astype(jnp.bfloat16)
        bra_state = propagate_one_body(sectioned, one_body)
    return bra_state
```

```python
import jax
import jax.numpy as jnp
from jax import lax
from jax.experimental import pallas as pl
from jax.experimental.pallas import tpu as pltpu
from jax.sharding import PartitionSpec as P

ORDER = 4
NORB = 104
TILES = 11
PER = 5
MESH = pl.DeviceIdType.MESH
F32, BF16 = jnp.float32, jnp.bfloat16


def place():
    walk, pb = lax.axis_index("walk"), lax.axis_index("pb")
    return walk, pb, walk // 2, lax.rem(walk, 2)


def moved(site, step):
    z = lax.rem(site // 2 + lax.rem(step, 8), 8)
    return z * 2 + lax.rem(lax.rem(site, 2) + step // 8, 2)


def tile_of(site, pb):
    spot = lax.rem(lax.rem(site, 2) * 8 + site // 2 + 2 * (pb // 4) + lax.rem(pb, 4), 16)
    return spot - (spot + 1) // 3, lax.rem(spot, 3) != 1


def lanes_of(shape):
    return lax.broadcasted_iota(jnp.int32, shape, len(shape) - 1)


def unflatten(ref, lead, mats, rows):
    for a in range(13):
        x = (ref[0, :, a * 1664 : (a + 1) * 1664] if lead else ref[:, a * 1664 : (a + 1) * 1664]).astype(F32)
        y = jnp.stack([x[:, 208 * i : 208 * (i + 1)] for i in range(8)], axis=0)
        mats[:, 8 * a : 8 * a + 8, 0:208] = jnp.transpose(y, (1, 0, 2))


def pack(mats, packed):
    lanes = lanes_of((16, 128))
    for g in range(PER):
        for b in range(6):
            packed[b, g] = mats[g, 16 * b : 16 * b + 16, 0:128].astype(BF16)
        tail = jnp.where(lanes[:8] < 64, mats[g, 96:104, 128:256], 0.0)
        packed[6, g] = jnp.concatenate([mats[g, 96:104, 0:128], tail], axis=0).astype(BF16)
        for m in range(3):
            even = mats[g, 32 * m : 32 * m + 16, 128:256]
            odd = mats[g, 32 * m + 16 : 32 * m + 32, 128:256]
            packed[7 + m, g] = jnp.where(lanes < 64, even, pltpu.roll(odd, 64, 1)).astype(BF16)
        last = jnp.zeros((16, 128), F32)
        for b in range(7):
            block = mats[g, 16 * b : 16 * b + 16, 128:256]
            if b == 6:
                block = jnp.where(lax.broadcasted_iota(jnp.int32, (16, 128), 0) < 8, block, 0.0)
            block = pltpu.roll(block, (16 * b - 64) % 128, 1)
            last = jnp.where((lanes >= 16 * b) & (lanes < 16 * b + 16), block, last)
        packed[10, g] = last.astype(BF16)


def unpack(hr, right, j):
    lanes = lanes_of((16, 128))
    last = hr[j * TILES + 10].astype(F32)
    for b in range(7):
        if b < 6:
            block = hr[j * TILES + 7 + b // 2].astype(F32)
            if b % 2:
                block = pltpu.roll(block, 64, 1)
        else:
            block = hr[j * TILES + 6].astype(F32)
            block = jnp.concatenate([block[8:16], jnp.zeros((8, 128), F32)], axis=0)
        end = pltpu.roll(last, (64 - 16 * b) % 128, 1)
        block = jnp.where(lanes < 64, block, jnp.where(lanes < 80, end, 0.0))
        right[j, 16 * b : 16 * b + 16] = block.astype(BF16)
    right[j, 112:128] = jnp.zeros((16, 128), BF16)


def complex_join(acc):
    keep = lanes_of((16, 128)) < NORB
    low, high = acc[:, 0:128], acc[:, 104:232]
    real = jnp.where(keep, low[0:16] - high[16:32], 0.0)
    imag = jnp.where(keep, high[0:16] + low[16:32], 0.0)
    return jnp.concatenate([real, imag], axis=0)


def kernel(
    chol, ftile, start, spread, one_body, out,
    mats, obm, packed, crecv, cmat, plain, hs, hr, right, obuf,
    csend, crec, fsend, frec, hsend, hrec, hloc, osend, orec, ready,
):
    walk, pb, site, core = place()
    tile, maker = tile_of(site, pb)
    active = pb // 8 == core
    mine = lax.rem(pb, 8)

    def remote(src, dst, send, rec, to_walk, to_pb):
        return pltpu.make_async_remote_copy(
            src_ref=src, dst_ref=dst, send_sem=send, recv_sem=rec,
            device_id=(to_walk, to_pb), device_id_type=MESH,
        )

    barrier = pltpu.get_barrier_semaphore()
    sibling = walk + 1 - 2 * core
    for i in range(1, 16):
        pl.semaphore_signal(barrier, inc=1, device_id=(moved(site, i) * 2 + core, pb), device_id_type=MESH)
        pl.semaphore_signal(barrier, inc=1, device_id=(walk, lax.rem(pb + i, 16)), device_id_type=MESH)
    pl.semaphore_signal(barrier, inc=1, device_id=(sibling, pb), device_id_type=MESH)

    unflatten(chol, True, mats, PER)
    pack(mats, packed)
    for t in range(TILES):
        packed[t, PER] = ftile[...]

    pl.semaphore_wait(barrier, 31)
    for i in range(1, 16):
        pl.semaphore_signal(ready, inc=1, device_id=(walk, lax.rem(pb + i, 16)), device_id_type=MESH)

    for i in range(1, 16):
        there = moved(site, i)
        t, makes = tile_of(there, pb)

        @pl.when(makes)
        def _():
            remote(packed.at[t], crecv.at[site], csend, crec, there * 2 + core, pb).start()

    @pl.when(maker)
    def _():
        crecv[site] = packed[tile]

    unflatten(one_body, False, obm, 4)
    pl.semaphore_wait(ready, 15)

    @pl.when(maker)
    def _():
        remote(packed.at[0:10], packed.at[0:10], csend, crec, sibling, pb).wait_send()
        remote(crecv.at[0:15], crecv.at[0:15], csend, crec, sibling, pb).wait_recv()
        for kg in range(5):
            block = jnp.stack([crecv[(16 * kg + i) // PER, (16 * kg + i) % PER].astype(F32) for i in range(16)], axis=0)
            block = jnp.transpose(block, (1, 0, 2)).astype(BF16)
            cmat[:, pl.ds(pl.multiple_of(core * 80 + 16 * kg, 16), 16), :] = block
        half = cmat.at[:, pl.ds(pl.multiple_of(core * 80, 16), 80), :]
        copy = remote(half, half, fsend, frec, sibling, pb)
        copy.start()
        ft = crecv[:, PER].astype(F32)
        f = jnp.concatenate([ft[:, 0:8].reshape(128, 128), ft[:, 8:16].reshape(128, 128)[:, 0:32]], axis=1).astype(BF16)
        copy.wait()
        for p in range(0, 16, 2):
            rhs = jnp.concatenate([cmat[p], cmat[p + 1]], axis=1)
            both = jnp.dot(f, rhs, preferred_element_type=F32)
            plain[p] = both[:, 0:128]
            plain[p + 1] = both[:, 128:256]

        def send(site_to, i_to):
            return remote(
                hs.at[site_to * 8 + i_to], hr.at[pb * TILES + tile], hsend, hrec, site_to * 2 + core, core * 8 + i_to
            )

        def lay(there):
            rows = pl.ds(pl.multiple_of(there * 8, 8), 8)
            hs[rows] = jnp.transpose(plain[:, rows, :], (1, 0, 2)).astype(BF16)

        lay(site)

        @pl.when(active)
        def _():
            pltpu.make_async_copy(hs.at[site * 8 + mine], hr.at[pb * TILES + tile], hloc).start()

        @pl.when(jnp.logical_not(active))
        def _():
            send(site, mine).start()

        for di in range(1, 8):
            send(site, lax.rem(mine + di, 8)).start()

        def block(step, carry):
            there = moved(site, step)
            lay(there)
            for di in range(8):
                send(there, lax.rem(mine + di, 8)).start()
            return carry

        lax.fori_loop(1, 16, block, 0)

        @pl.when(active)
        def _():
            pltpu.make_async_copy(hs.at[site * 8 + mine], hr.at[pb * TILES + tile], hloc).wait()
            remote(hs.at[0:127], hs.at[0:127], hsend, hrec, sibling, pb).wait_send()

        @pl.when(jnp.logical_not(active))
        def _():
            remote(hs, hs, hsend, hrec, sibling, pb).wait_send()

    @pl.when(jnp.logical_not(maker))
    def _():
        remote(packed, packed, csend, crec, sibling, pb).wait_send()

    @pl.when(active)
    def _():
        @pl.when(maker)
        def _():
            remote(hr.at[0:175], hr.at[0:175], hsend, hrec, sibling, pb).wait_recv()

        @pl.when(jnp.logical_not(maker))
        def _():
            remote(hr, hr, hsend, hrec, sibling, pb).wait_recv()

        for j in range(16):
            unpack(hr, right, j)
        current = start[...]
        summed = current.astype(F32)
        for n in range(1, ORDER + 1):
            lhs = jnp.dot(spread[...], current, preferred_element_type=F32).astype(BF16)
            acc = jnp.zeros((32, 256), F32)
            for j in range(0, 16, 2):
                mats2 = [
                    jnp.concatenate([hr[i * TILES : i * TILES + 8].reshape(128, 128), right[i]], axis=1)
                    for i in (j, j + 1)
                ]
                rows2 = jnp.concatenate([lhs[32 * j : 32 * j + 32], lhs[32 * j + 32 : 32 * j + 64]], axis=1)
                acc += jnp.dot(rows2, jnp.concatenate(mats2, axis=0), preferred_element_type=F32)
            scaled = complex_join(acc) / float(n)
            summed = summed + scaled
            current = scaled.astype(BF16)
        section = summed.astype(BF16)
        kpoint = lax.rem(lax.broadcasted_iota(jnp.int32, (32, NORB), 0), 16) // 4
        acc = jnp.zeros((32, 256), F32)
        for k in range(4):
            rows = jnp.where(kpoint == k, section[:, 0:NORB].astype(F32), 0.0).astype(BF16)
            acc += jnp.dot(rows, obm[k].astype(BF16), preferred_element_type=F32)
        joined = complex_join(acc)
        zero = jnp.zeros((16, 128), F32)
        wide = jnp.concatenate([joined[0:16], zero], axis=1)
        wide += pltpu.roll(jnp.concatenate([joined[16:32], zero], axis=1), NORB, 1)
        obuf[mine] = wide.astype(BF16)
        for i in range(1, 16):
            remote(obuf.at[mine], obuf.at[mine], osend, orec, walk, lax.rem(pb + i, 16)).start()
        remote(obuf.at[0:7], obuf.at[0:7], osend, orec, sibling, pb).wait_recv()
        remote(hs.at[0:30], hs.at[0:30], osend, orec, sibling, pb).wait_send()

    @pl.when(jnp.logical_not(active))
    def _():
        remote(obuf, obuf, osend, orec, sibling, pb).wait_recv()

    out[...] = obuf[:, :, 0 : 2 * NORB]


def shards(bras, fields, chol, one_body, pair_table, kpq_map):
    walkers, kpoints, occupied, doubled = bras.shape
    pb = lax.axis_index("pb")
    charge = lax.dynamic_index_in_dim(pair_table[:, 0], pb, keepdims=False)
    f = lax.dynamic_index_in_dim(fields[0], charge, axis=1, keepdims=False)
    f = f.reshape(walkers, 16, 2, PER).transpose(0, 2, 1, 3).reshape(walkers, 160).astype(BF16)
    ftile = jnp.concatenate([f[:, 0:128], jnp.pad(f[:, 128:160], ((0, 0), (0, 96)))], axis=0)
    bra = lax.dynamic_index_in_dim(bras, lax.rem(pb, 8), keepdims=False)
    bra = bra.reshape(16, 2, NORB).transpose(1, 0, 2).reshape(32, NORB)
    start = jnp.pad(bra, ((0, 0), (0, 128 - NORB)))
    levels = jnp.arange(kpoints, dtype=jnp.int32)
    from_hot = (pair_table[:, 1:2] == levels).astype(jnp.int32)
    charge_hot = (pair_table[:, 0:1] == levels).astype(jnp.int32)
    target = jnp.sum(charge_hot[:, :, None] * from_hot[:, None, :] * kpq_map[None], axis=(1, 2))
    to_hot = (target[:, None] == levels).astype(jnp.int32)
    hot = to_hot[:, :, None] * from_hot[:, None, :]
    row = jnp.arange(32)
    same = (row[:, None] // 16 == row[None, :] // 16) & (row[:, None] % 4 == row[None, :] % 4)
    kp = row % 16 // 4
    spread = jnp.where(same[None], jnp.take(jnp.take(hot, kp, axis=1), kp, axis=2), 0)
    spread = spread.reshape(512, 32).astype(BF16)

    vmem = pl.BlockSpec(memory_space=pltpu.VMEM)
    dma = pltpu.SemaphoreType.DMA(())
    new = pl.pallas_call(
        kernel,
        out_shape=jax.ShapeDtypeStruct((walkers, 16, doubled), BF16),
        in_specs=[vmem] * 5,
        out_specs=vmem,
        scratch_shapes=[
            pltpu.VMEM((PER, 112, 256), F32),
            pltpu.VMEM((4, NORB, 256), F32),
            pltpu.VMEM((TILES, PER + 1, 16, 128), BF16),
            pltpu.VMEM((16, PER + 1, 16, 128), BF16),
            pltpu.VMEM((16, 160, 128), BF16),
            pltpu.VMEM((16, 128, 128), F32),
            pltpu.VMEM((128, 16, 128), BF16),
            pltpu.VMEM((16 * TILES, 16, 128), BF16),
            pltpu.VMEM((16, 128, 128), BF16),
            pltpu.VMEM((8, 16, 256), BF16),
            *[dma] * 9,
            pltpu.SemaphoreType.REGULAR,
        ],
        compiler_params=pltpu.CompilerParams(
            collective_id=0, has_side_effects=True, vmem_limit_bytes=32 * 2**20
        ),
        cost_estimate=pl.CostEstimate(flops=10**8, bytes_accessed=10**6, transcendentals=0),
    )(chol, ftile, start, spread, one_body)
    return new.reshape(walkers, kpoints, occupied, doubled)


def solution(mesh):
    return jax.shard_map(
        shards,
        mesh=mesh,
        in_specs=(
            P("walk", None, None, None),
            P(None, "walk", None, None),
            P("pb", "walk", None),
            P(),
            P(),
            P(),
        ),
        out_specs=P("walk", None, None, None),
        check_vma=False,
    )
```

```python
import jax
import jax.numpy as jnp
from jax import lax
from jax.experimental import pallas as pl
from jax.experimental.pallas import tpu as pltpu
from jax.sharding import PartitionSpec as P

ORDER = 4
NORB = 104
TILES = 11
PER = 5
FAR = (12, 11, 13, 4, 10, 14, 3, 5, 9, 15, 2, 6, 8, 1, 7, 0)
ORDER_SITES = (0, 2, 1, 4, 3, 6, 5, 8, 7, 10, 12, 14, 9, 11, 13, 15)
MESH = pl.DeviceIdType.MESH
F32, BF16 = jnp.float32, jnp.bfloat16


def place():
    walk, pb = lax.axis_index("walk"), lax.axis_index("pb")
    return walk, pb, walk // 2, lax.rem(walk, 2)


def moved(site, step):
    z = lax.rem(site // 2 + lax.rem(step, 8), 8)
    return z * 2 + lax.rem(lax.rem(site, 2) + step // 8, 2)


def tile_of(site, pb):
    spot = lax.rem(lax.rem(site, 2) * 8 + site // 2 + 2 * (pb // 4) + lax.rem(pb, 4), 16)
    return spot - (spot + 1) // 3, lax.rem(spot, 3) != 1, lax.rem(site // 2 + pb, 2)


def lanes_of(shape):
    return lax.broadcasted_iota(jnp.int32, shape, len(shape) - 1)


def unflatten(ref, lead, mats, rows):
    for a in range(13):
        x = (ref[0, :, a * 1664 : (a + 1) * 1664] if lead else ref[:, a * 1664 : (a + 1) * 1664]).astype(F32)
        y = jnp.stack([x[:, 208 * i : 208 * (i + 1)] for i in range(8)], axis=0)
        mats[:, 8 * a : 8 * a + 8, 0:208] = jnp.transpose(y, (1, 0, 2))


def pack(mats, packed):
    lanes = lanes_of((16, 128))
    for g in range(PER):
        for b in range(6):
            packed[b, g] = mats[g, 16 * b : 16 * b + 16, 0:128].astype(BF16)
        tail = jnp.where(lanes[:8] < 64, mats[g, 96:104, 128:256], 0.0)
        packed[6, g] = jnp.concatenate([mats[g, 96:104, 0:128], tail], axis=0).astype(BF16)
        for m in range(3):
            even = mats[g, 32 * m : 32 * m + 16, 128:256]
            odd = mats[g, 32 * m + 16 : 32 * m + 32, 128:256]
            packed[7 + m, g] = jnp.where(lanes < 64, even, pltpu.roll(odd, 64, 1)).astype(BF16)
        last = jnp.zeros((16, 128), F32)
        for b in range(7):
            block = mats[g, 16 * b : 16 * b + 16, 128:256]
            if b == 6:
                block = jnp.where(lax.broadcasted_iota(jnp.int32, (16, 128), 0) < 8, block, 0.0)
            block = pltpu.roll(block, (16 * b - 64) % 128, 1)
            last = jnp.where((lanes >= 16 * b) & (lanes < 16 * b + 16), block, last)
        packed[10, g] = last.astype(BF16)


def unpack(hr, right, j):
    lanes = lanes_of((16, 128))
    last = hr[j * TILES + 10].astype(F32)
    for b in range(7):
        if b < 6:
            block = hr[j * TILES + 7 + b // 2].astype(F32)
            if b % 2:
                block = pltpu.roll(block, 64, 1)
        else:
            block = hr[j * TILES + 6].astype(F32)
            block = jnp.concatenate([block[8:16], jnp.zeros((8, 128), F32)], axis=0)
        end = pltpu.roll(last, (64 - 16 * b) % 128, 1)
        block = jnp.where(lanes < 64, block, jnp.where(lanes < 80, end, 0.0))
        right[j, 16 * b : 16 * b + 16] = block.astype(BF16)
    right[j, 112:128] = jnp.zeros((16, 128), BF16)


def complex_join(acc):
    keep = lanes_of((16, 128)) < NORB
    low, high = acc[:, 0:128], acc[:, 104:232]
    real = jnp.where(keep, low[0:16] - high[16:32], 0.0)
    imag = jnp.where(keep, high[0:16] + low[16:32], 0.0)
    return jnp.concatenate([real, imag], axis=0)


def field_tile(fields, charge):
    f = jnp.zeros((8, 160), F32)
    for q in range(4):
        f = jnp.where(charge == q, fields[0, :, q, :], f)
    rest = jnp.concatenate([f[:, 128:160], jnp.zeros((8, 96), F32)], axis=1)
    return jnp.concatenate([f[:, 0:128], rest], axis=0).astype(BF16)


def spread_rows(pairs, kpq, spread):
    row = lax.broadcasted_iota(jnp.int32, (32, 32), 0)
    col = lax.broadcasted_iota(jnp.int32, (32, 32), 1)
    same = (row // 16 == col // 16) & (row % 4 == col % 4)
    row, col = row % 16 // 4, col % 16 // 4
    for j in range(16):
        source = pairs[1, j]
        target = kpq[pairs[0, j], source]
        spread[32 * j : 32 * j + 32] = jnp.where(same & (row == target) & (col == source), 1.0, 0.0).astype(BF16)


def split_rows(bras, mine):
    rows = jnp.concatenate([bras[mine, k].astype(F32) for k in range(4)], axis=0)
    wide = jnp.concatenate([rows, jnp.zeros((16, 48), F32)], axis=1)
    keep = lanes_of((16, 128)) < NORB
    halves = [jnp.where(keep, wide[:, 0:128], 0.0), jnp.where(keep, wide[:, NORB : NORB + 128], 0.0)]
    return jnp.concatenate(halves, axis=0)


def kernel(
    bras_in, fields_in, chol_in, one_body_in, pairs, kpq, out,
    bras, fields, chol, one_body, spread,
    mats, obm, packed, crecv, cmat, plain, hs, hr, right, obuf,
    load, csend, crec, hsend, hrec, hloc, osend, orec, ready,
):
    walk, pb, site, core = place()
    tile, makes, maker_core = tile_of(site, pb)
    maker = makes & (maker_core == core)
    active = pb // 8 != core
    mine = lax.rem(pb, 8)

    def remote(src, dst, send, rec, to_walk, to_pb):
        return pltpu.make_async_remote_copy(
            src_ref=src, dst_ref=dst, send_sem=send, recv_sem=rec,
            device_id=(to_walk, to_pb), device_id_type=MESH,
        )

    loads = [
        pltpu.make_async_copy(src, dst, load.at[i])
        for i, (src, dst) in enumerate([(chol_in, chol), (fields_in, fields), (one_body_in, one_body), (bras_in, bras)])
    ]
    for copy in loads:
        copy.start()
    barrier = pltpu.get_barrier_semaphore()
    sibling = walk + 1 - 2 * core
    for i in FAR:
        for c in (0, 1) if i else (1,):
            to = moved(site, i) * 2 + lax.rem(core + c, 2)
            pl.semaphore_signal(barrier, inc=1, device_id=(to, pb), device_id_type=MESH)
    for i in range(1, 16):
        pl.semaphore_signal(barrier, inc=1, device_id=(walk, lax.rem(pb + i, 16)), device_id_type=MESH)

    loads[0].wait()
    unflatten(chol, True, mats, PER)
    pack(mats, packed)
    loads[1].wait()
    ftile = field_tile(fields, pairs[0, pb])
    for t in range(TILES):
        packed[t, PER] = ftile

    pl.semaphore_wait(barrier, 46)
    for i in range(1, 16):
        pl.semaphore_signal(ready, inc=1, device_id=(walk, lax.rem(pb + i, 16)), device_id_type=MESH)

    for i in FAR:
        there = moved(site, i)
        t, used, c = tile_of(there, pb)

        @pl.when(used & ((c != core) if i == 0 else True))
        def _():
            remote(packed.at[t], crecv.at[walk], csend, crec, there * 2 + c, pb).start()

    @pl.when(maker)
    def _():
        crecv[walk] = packed[tile]

    loads[2].wait()
    unflatten(one_body, False, obm, 4)
    spread_rows(pairs, kpq, spread)
    loads[3].wait()
    pl.semaphore_wait(ready, 15)

    @pl.when(maker)
    def _():
        remote(crecv.at[0:31], crecv.at[0:31], csend, crec, sibling, pb).wait_recv()
        for kg in range(10):
            block = jnp.stack([crecv[(16 * kg + i) // PER, (16 * kg + i) % PER].astype(F32) for i in range(16)], axis=0)
            cmat[:, 16 * kg : 16 * kg + 16, :] = jnp.transpose(block, (1, 0, 2)).astype(BF16)
        ft = crecv[:, PER].astype(F32)
        f = jnp.concatenate([ft[:, 0:8].reshape(256, 128), ft[:, 8:16].reshape(256, 128)[:, 0:32]], axis=1).astype(BF16)
        for p in range(0, 16, 2):
            rhs = jnp.concatenate([cmat[p], cmat[p + 1]], axis=1)
            both = jnp.dot(f, rhs, preferred_element_type=F32)
            plain[p] = both[:, 0:128]
            plain[p + 1] = both[:, 128:256]

        def send(to, i):
            return remote(hs.at[to * 8 + i], hr.at[pb * TILES + tile], hsend, hrec, to, 8 - lax.rem(to, 2) * 8 + i)

        for to in range(32):
            hs[8 * to : 8 * to + 8] = jnp.transpose(plain[:, 8 * to : 8 * to + 8, :], (1, 0, 2)).astype(BF16)

        @pl.when(active)
        def _():
            pltpu.make_async_copy(hs.at[walk * 8 + mine], hr.at[pb * TILES + tile], hloc).start()

        for there in ORDER_SITES:
            for to in (2 * there, 2 * there + 1):

                @pl.when((to != walk) | jnp.logical_not(active))
                def _():
                    send(to, mine).start()

                def rest(di, carry):
                    send(to, lax.rem(mine + di, 8)).start()
                    return carry

                lax.fori_loop(1, 8, rest, 0)

    @pl.when(active)
    def _():
        @pl.when(maker)
        def _():
            pltpu.make_async_copy(hs.at[walk * 8 + mine], hr.at[pb * TILES + tile], hloc).wait()
            remote(hr.at[0:175], hr.at[0:175], hsend, hrec, sibling, pb).wait_recv()

        @pl.when(jnp.logical_not(maker))
        def _():
            remote(hr, hr, hsend, hrec, sibling, pb).wait_recv()

        for j in range(16):
            unpack(hr, right, j)
        summed = split_rows(bras, mine)
        current = summed.astype(BF16)
        for n in range(1, ORDER + 1):
            lhs = jnp.dot(spread[...], current, preferred_element_type=F32).astype(BF16)
            acc = jnp.zeros((32, 256), F32)
            for j in range(0, 16, 2):
                mats2 = [
                    jnp.concatenate([hr[i * TILES : i * TILES + 8].reshape(128, 128), right[i]], axis=1)
                    for i in (j, j + 1)
                ]
                rows2 = jnp.concatenate([lhs[32 * j : 32 * j + 32], lhs[32 * j + 32 : 32 * j + 64]], axis=1)
                acc += jnp.dot(rows2, jnp.concatenate(mats2, axis=0), preferred_element_type=F32)
            scaled = complex_join(acc) / float(n)
            summed = summed + scaled
            current = scaled.astype(BF16)
        section = summed.astype(BF16)
        kpoint = lax.rem(lax.broadcasted_iota(jnp.int32, (32, NORB), 0), 16) // 4
        acc = jnp.zeros((32, 256), F32)
        for k in range(4):
            rows = jnp.where(kpoint == k, section[:, 0:NORB].astype(F32), 0.0).astype(BF16)
            acc += jnp.dot(rows, obm[k].astype(BF16), preferred_element_type=F32)
        joined = complex_join(acc)
        zero = jnp.zeros((16, 128), F32)
        wide = jnp.concatenate([joined[0:16], zero], axis=1)
        wide += pltpu.roll(jnp.concatenate([joined[16:32], zero], axis=1), NORB, 1)
        obuf[mine] = wide.astype(BF16)
        for i in range(1, 16):
            remote(obuf.at[mine], obuf.at[mine], osend, orec, walk, lax.rem(pb + i, 16)).start()
        remote(obuf.at[0:7], obuf.at[0:7], osend, orec, sibling, pb).wait_recv()

    @pl.when(jnp.logical_not(active))
    def _():
        remote(obuf, obuf, osend, orec, sibling, pb).wait_recv()

    @pl.when(maker)
    def _():
        remote(packed.at[0:10], packed.at[0:10], csend, crec, sibling, pb).wait_send()

        @pl.when(active)
        def _():
            remote(hs.at[0:255], hs.at[0:255], hsend, hrec, sibling, pb).wait_send()

        @pl.when(jnp.logical_not(active))
        def _():
            remote(hs, hs, hsend, hrec, sibling, pb).wait_send()

    @pl.when(jnp.logical_not(maker))
    def _():
        remote(packed, packed, csend, crec, sibling, pb).wait_send()

    @pl.when(active)
    def _():
        remote(hs.at[0:30], hs.at[0:30], osend, orec, sibling, pb).wait_send()

    for w in range(8):
        rows = obuf[w].astype(F32)
        for k in range(4):
            out[w, k] = rows[4 * k : 4 * k + 4, 0 : 2 * NORB].astype(BF16)


def shards(bras, fields, chol, one_body, pair_table, kpq_map):
    anywhere, smem = pl.BlockSpec(memory_space=pltpu.HBM), pl.BlockSpec(memory_space=pltpu.SMEM)
    dma = pltpu.SemaphoreType.DMA(())
    return pl.pallas_call(
        kernel,
        out_shape=jax.ShapeDtypeStruct(bras.shape, BF16),
        in_specs=[anywhere] * 4 + [smem] * 2,
        out_specs=pl.BlockSpec(memory_space=pltpu.VMEM),
        scratch_shapes=[
            pltpu.VMEM(bras.shape, BF16),
            pltpu.VMEM(fields.shape, F32),
            pltpu.VMEM(chol.shape, BF16),
            pltpu.VMEM(one_body.shape, BF16),
            pltpu.VMEM((512, 32), BF16),
            pltpu.VMEM((PER, 112, 256), F32),
            pltpu.VMEM((4, NORB, 256), F32),
            pltpu.VMEM((TILES, PER + 1, 16, 128), BF16),
            pltpu.VMEM((32, PER + 1, 16, 128), BF16),
            pltpu.VMEM((16, 160, 128), BF16),
            pltpu.VMEM((16, 256, 128), F32),
            pltpu.VMEM((256, 16, 128), BF16),
            pltpu.VMEM((16 * TILES, 16, 128), BF16),
            pltpu.VMEM((16, 128, 128), BF16),
            pltpu.VMEM((8, 16, 256), BF16),
            pltpu.SemaphoreType.DMA((4,)),
            *[dma] * 7,
            pltpu.SemaphoreType.REGULAR,
        ],
        compiler_params=pltpu.CompilerParams(
            collective_id=0, has_side_effects=True, vmem_limit_bytes=60 * 2**20
        ),
        cost_estimate=pl.CostEstimate(flops=10**8, bytes_accessed=10**6, transcendentals=0),
    )(bras, fields, chol, one_body, pair_table.T, kpq_map)


def solution(mesh):
    return jax.shard_map(
        shards,
        mesh=mesh,
        in_specs=(
            P("walk", None, None, None),
            P(None, "walk", None, None),
            P("pb", "walk", None),
            P(),
            P(),
            P(),
        ),
        out_specs=P("walk", None, None, None),
        check_vma=False,
    )
```

```python
import jax
import jax.numpy as jnp
from jax import lax
from jax.experimental import pallas as pl
from jax.experimental.pallas import tpu as pltpu
from jax.sharding import PartitionSpec as P

ORDER = 4
NORB = 104
TILES = 11
PER = 5
FAR = (12, 11, 13, 4, 10, 14, 3, 5, 9, 15, 2, 6, 8, 1, 7, 0)
BLOCKS = ((0, 64, (0, 2, 1, 3)), (64, 256, (4, 6, 5, 8, 7, 10, 12, 14, 9, 11, 13, 15)))
MESH = pl.DeviceIdType.MESH
F32, BF16 = jnp.float32, jnp.bfloat16


def place():
    walk, pb = lax.axis_index("walk"), lax.axis_index("pb")
    return walk, pb, walk // 2, lax.rem(walk, 2)


def moved(site, step):
    z = lax.rem(site // 2 + lax.rem(step, 8), 8)
    return z * 2 + lax.rem(lax.rem(site, 2) + step // 8, 2)


def tile_of(site, pb):
    spot = lax.rem(lax.rem(site, 2) * 8 + site // 2 + 2 * (pb // 4) + lax.rem(pb, 4), 16)
    return spot - (spot + 1) // 3, lax.rem(spot, 3) != 1, lax.rem(site // 2 + pb, 2)


def lanes_of(shape):
    return lax.broadcasted_iota(jnp.int32, shape, len(shape) - 1)


def unflatten(ref, lead, mats, rows):
    for a in range(13):
        x = (ref[0, :, a * 1664 : (a + 1) * 1664] if lead else ref[:, a * 1664 : (a + 1) * 1664]).astype(F32)
        y = jnp.stack([x[:, 208 * i : 208 * (i + 1)] for i in range(8)], axis=0)
        mats[:, 8 * a : 8 * a + 8, 0:208] = jnp.transpose(y, (1, 0, 2))


def pack(mats, packed):
    lanes = lanes_of((16, 128))
    for g in range(PER):
        for b in range(6):
            packed[b, g] = mats[g, 16 * b : 16 * b + 16, 0:128].astype(BF16)
        tail = jnp.where(lanes[:8] < 64, mats[g, 96:104, 128:256], 0.0)
        packed[6, g] = jnp.concatenate([mats[g, 96:104, 0:128], tail], axis=0).astype(BF16)
        for m in range(3):
            even = mats[g, 32 * m : 32 * m + 16, 128:256]
            odd = mats[g, 32 * m + 16 : 32 * m + 32, 128:256]
            packed[7 + m, g] = jnp.where(lanes < 64, even, pltpu.roll(odd, 64, 1)).astype(BF16)
        last = jnp.zeros((16, 128), F32)
        for b in range(7):
            block = mats[g, 16 * b : 16 * b + 16, 128:256]
            if b == 6:
                block = jnp.where(lax.broadcasted_iota(jnp.int32, (16, 128), 0) < 8, block, 0.0)
            block = pltpu.roll(block, (16 * b - 64) % 128, 1)
            last = jnp.where((lanes >= 16 * b) & (lanes < 16 * b + 16), block, last)
        packed[10, g] = last.astype(BF16)


def unpack(hr, right, j):
    lanes = lanes_of((16, 128))
    last = hr[j * TILES + 10].astype(F32)
    for b in range(7):
        if b < 6:
            block = hr[j * TILES + 7 + b // 2].astype(F32)
            if b % 2:
                block = pltpu.roll(block, 64, 1)
        else:
            block = hr[j * TILES + 6].astype(F32)
            block = jnp.concatenate([block[8:16], jnp.zeros((8, 128), F32)], axis=0)
        end = pltpu.roll(last, (64 - 16 * b) % 128, 1)
        block = jnp.where(lanes < 64, block, jnp.where(lanes < 80, end, 0.0))
        right[j, 16 * b : 16 * b + 16] = block.astype(BF16)
    right[j, 112:128] = jnp.zeros((16, 128), BF16)


def complex_join(acc):
    keep = lanes_of((4, 128)) < NORB
    low, high = acc[:, 0:128], acc[:, NORB : NORB + 128]
    return jnp.where(keep, low[0:4] - high[4:8], 0.0), jnp.where(keep, high[0:4] + low[4:8], 0.0)


def as_rows(rows):
    return jnp.concatenate([rows, jnp.zeros((8, 128), F32)], axis=0).astype(BF16)


def field_tile(fields, charge):
    f = jnp.zeros((8, 160), F32)
    for q in range(4):
        f = jnp.where(charge == q, fields[0, :, q, :], f)
    rest = jnp.concatenate([f[:, 128:160], jnp.zeros((8, 96), F32)], axis=1)
    return jnp.concatenate([f[:, 0:128], rest], axis=0).astype(BF16)


def split_rows(bras, mine, k):
    wide = jnp.concatenate([bras[mine, k].astype(F32), jnp.zeros((4, 48), F32)], axis=1)
    keep = lanes_of((4, 128)) < NORB
    halves = [jnp.where(keep, wide[:, i : i + 128], 0.0) for i in (0, NORB)]
    return jnp.concatenate(halves, axis=0)


def kernel(
    bras_in, fields_in, chol_in, one_body_in, pairs_in, kpq_in, out,
    bras, fields, chol, one_body, pairs, kpq,
    mats, obm, propagator, packed, crecv, cmat, plain, hs, hr, right, current, obuf,
    load, hrec, csend, crec, hsend, hloc, osend, orec, ready,
):
    walk, pb, site, core = place()
    tile, makes, maker_core = tile_of(site, pb)
    maker = makes & (maker_core == core)
    active = pb // 8 != core
    mine = lax.rem(pb, 8)

    def remote(src, dst, send, rec, to_walk, to_pb):
        return pltpu.make_async_remote_copy(
            src_ref=src, dst_ref=dst, send_sem=send, recv_sem=rec,
            device_id=(to_walk, to_pb), device_id_type=MESH,
        )

    loads = [
        pltpu.make_async_copy(src, dst, load.at[i])
        for i, (src, dst) in enumerate(
            [(chol_in, chol), (fields_in, fields), (one_body_in, one_body)]
            + [(bras_in, bras), (pairs_in, pairs), (kpq_in, kpq)]
        )
    ]
    barrier = pltpu.get_barrier_semaphore()
    sibling = walk + 1 - 2 * core
    for i in FAR:
        for c in (0, 1) if i else (1,):
            to = moved(site, i) * 2 + lax.rem(core + c, 2)
            pl.semaphore_signal(barrier, inc=1, device_id=(to, pb), device_id_type=MESH)
    for i in range(1, 16):
        pl.semaphore_signal(barrier, inc=1, device_id=(walk, lax.rem(pb + i, 16)), device_id_type=MESH)

    for copy in loads:
        copy.start()
    loads[0].wait()
    unflatten(chol, True, mats, PER)
    pack(mats, packed)
    loads[1].wait()
    loads[4].wait()
    ftile = field_tile(fields, pairs[0, pb])
    for t in range(TILES):
        packed[t, PER] = ftile

    hands = []
    for i in FAR:
        there = moved(site, i)
        t, used, c = tile_of(there, pb)
        hands.append((there, t, used & (c != core) if i == 0 else used, c))
    pl.semaphore_wait(barrier, 46)
    for i in range(1, 16):
        pl.semaphore_signal(ready, inc=1, device_id=(walk, lax.rem(pb + i, 16)), device_id_type=MESH)

    for there, t, used, c in hands:

        @pl.when(used)
        def _():
            remote(packed.at[t], crecv.at[walk], csend, crec, there * 2 + c, pb).start()

    @pl.when(maker)
    def _():
        crecv[walk] = packed[tile]

    loads[2].wait()
    unflatten(one_body, False, obm, 4)
    for k in range(4):
        obm[k, NORB:112] = jnp.zeros((8, 256), F32)
        propagator[k, 0:112] = obm[k].astype(BF16)
        propagator[k, 112:128] = jnp.zeros((16, 256), BF16)
    loads[3].wait()
    loads[5].wait()
    pl.semaphore_wait(ready, 15)

    @pl.when(maker)
    def _():
        remote(crecv.at[0:31], crecv.at[0:31], csend, crec, sibling, pb).wait_recv()
        for kg in range(10):
            block = jnp.stack([crecv[(16 * kg + i) // PER, (16 * kg + i) % PER].astype(F32) for i in range(16)], axis=0)
            cmat[:, 16 * kg : 16 * kg + 16, :] = jnp.transpose(block, (1, 0, 2)).astype(BF16)
        ft = crecv[:, PER].astype(F32)
        f = jnp.concatenate([ft[:, 0:8].reshape(256, 128), ft[:, 8:16].reshape(256, 128)[:, 0:32]], axis=1).astype(BF16)
        def send(to, i):
            return remote(hs.at[to * 8 + i], hr.at[pb * TILES + tile], hsend, hrec.at[pb // 4], to, 8 - lax.rem(to, 2) * 8 + i)

        for start, stop, sites in BLOCKS:
            for p in range(0, 16, 2):
                rhs = jnp.concatenate([cmat[p], cmat[p + 1]], axis=1)
                both = jnp.dot(f[start:stop], rhs, preferred_element_type=F32)
                plain[p, start:stop] = both[:, 0:128]
                plain[p + 1, start:stop] = both[:, 128:256]
            for to in range(start // 8, stop // 8):
                hs[8 * to : 8 * to + 8] = jnp.transpose(plain[:, 8 * to : 8 * to + 8, :], (1, 0, 2)).astype(BF16)
            for there in sites:
                for to in (2 * there, 2 * there + 1):

                    @pl.when((to != walk) | jnp.logical_not(active))
                    def _():
                        send(to, mine).start()

                    def rest(di, carry):
                        send(to, lax.rem(mine + di, 8)).start()
                        return carry

                    lax.fori_loop(1, 8, rest, 0)

        @pl.when(active)
        def _():
            pltpu.make_async_copy(hs.at[walk * 8 + mine], hr.at[pb * TILES + tile], hloc).start()

    @pl.when(active)
    def _():
        sources = [pairs[1, j] for j in range(16)]
        targets = [kpq[pairs[0, j], sources[j]] for j in range(16)]
        summed = [split_rows(bras, mine, k) for k in range(4)]
        for k in range(4):
            current[k] = as_rows(summed[k])

        def arrived(group, ones):
            some = hr.at[pl.ds(group * 4 * TILES, ones)]
            return remote(some, some, hsend, hrec.at[group], sibling, pb)

        @pl.when(maker)
        def _():
            pltpu.make_async_copy(hs.at[walk * 8 + mine], hr.at[pb * TILES + tile], hloc).wait()

        for n in range(1, ORDER + 1):
            acc = [jnp.zeros((8, 256), F32) for _ in range(4)]
            for j in range(16):
                if n == 1 and j % 4 == 0:
                    own = maker & (pb // 4 == j // 4)

                    @pl.when(own)
                    def _():
                        arrived(j // 4, 4 * TILES - 1).wait_recv()

                    @pl.when(jnp.logical_not(own))
                    def _():
                        arrived(j // 4, 4 * TILES).wait_recv()

                if n == 1:
                    unpack(hr, right, j)
                matrix = jnp.concatenate([hr[j * TILES : j * TILES + 8].reshape(128, 128), right[j]], axis=1)
                product = jnp.dot(current[sources[j]], matrix, preferred_element_type=F32)[0:8]
                acc = [acc[k] + jnp.where(targets[j] == k, product, 0.0) for k in range(4)]
            for k in range(4):
                scaled = jnp.concatenate(complex_join(acc[k]), axis=0) * (1.0 / n)
                summed[k] = summed[k] + scaled
                current[k] = as_rows(scaled)
        joined = [
            complex_join(jnp.dot(as_rows(summed[k]), propagator[k], preferred_element_type=F32)) for k in range(4)
        ]
        real, imag = (jnp.concatenate([one[i] for one in joined], axis=0) for i in (0, 1))
        zero = jnp.zeros((16, 128), F32)
        wide = jnp.concatenate([real, zero], axis=1)
        wide += pltpu.roll(jnp.concatenate([imag, zero], axis=1), NORB, 1)
        obuf[mine] = wide.astype(BF16)
        for i in range(1, 16):
            remote(obuf.at[mine], obuf.at[mine], osend, orec, walk, lax.rem(pb + i, 16)).start()
        remote(obuf.at[0:7], obuf.at[0:7], osend, orec, sibling, pb).wait_recv()

    @pl.when(jnp.logical_not(active))
    def _():
        remote(obuf, obuf, osend, orec, sibling, pb).wait_recv()

    @pl.when(maker)
    def _():
        remote(packed.at[0:10], packed.at[0:10], csend, crec, sibling, pb).wait_send()

        @pl.when(active)
        def _():
            remote(hs.at[0:255], hs.at[0:255], hsend, hrec.at[0], sibling, pb).wait_send()

        @pl.when(jnp.logical_not(active))
        def _():
            remote(hs, hs, hsend, hrec.at[0], sibling, pb).wait_send()

    @pl.when(jnp.logical_not(maker))
    def _():
        remote(packed, packed, csend, crec, sibling, pb).wait_send()

    @pl.when(active)
    def _():
        remote(hs.at[0:30], hs.at[0:30], osend, orec, sibling, pb).wait_send()

    for w in range(8):
        rows = obuf[w].astype(F32)
        for k in range(4):
            out[w, k] = rows[4 * k : 4 * k + 4, 0 : 2 * NORB].astype(BF16)


def shards(bras, fields, chol, one_body, pair_table, kpq_map):
    dma = pltpu.SemaphoreType.DMA(())
    return pl.pallas_call(
        kernel,
        out_shape=jax.ShapeDtypeStruct(bras.shape, BF16),
        in_specs=[pl.BlockSpec(memory_space=pltpu.HBM)] * 6,
        out_specs=pl.BlockSpec(memory_space=pltpu.VMEM),
        scratch_shapes=[
            pltpu.VMEM(bras.shape, BF16),
            pltpu.VMEM(fields.shape, F32),
            pltpu.VMEM(chol.shape, BF16),
            pltpu.VMEM(one_body.shape, BF16),
            pltpu.SMEM((2, 16), jnp.int32),
            pltpu.SMEM((4, 4), jnp.int32),
            pltpu.VMEM((PER, 112, 256), F32),
            pltpu.VMEM((4, 112, 256), F32),
            pltpu.VMEM((4, 128, 256), BF16),
            pltpu.VMEM((TILES, PER + 1, 16, 128), BF16),
            pltpu.VMEM((32, PER + 1, 16, 128), BF16),
            pltpu.VMEM((16, 160, 128), BF16),
            pltpu.VMEM((16, 256, 128), F32),
            pltpu.VMEM((256, 16, 128), BF16),
            pltpu.VMEM((16 * TILES, 16, 128), BF16),
            pltpu.VMEM((16, 128, 128), BF16),
            pltpu.VMEM((4, 16, 128), BF16),
            pltpu.VMEM((8, 16, 256), BF16),
            pltpu.SemaphoreType.DMA((6,)),
            pltpu.SemaphoreType.DMA((4,)),
            *[dma] * 6,
            pltpu.SemaphoreType.REGULAR,
        ],
        compiler_params=pltpu.CompilerParams(
            collective_id=0, has_side_effects=True, vmem_limit_bytes=60 * 2**20
        ),
        cost_estimate=pl.CostEstimate(flops=10**8, bytes_accessed=10**6, transcendentals=0),
    )(bras, fields, chol, one_body, pair_table.T, kpq_map)


def solution(mesh):
    return jax.shard_map(
        shards,
        mesh=mesh,
        in_specs=(
            P("walk", None, None, None),
            P(None, "walk", None, None),
            P("pb", "walk", None),
            P(),
            P(),
            P(),
        ),
        out_specs=P("walk", None, None, None),
        check_vma=False,
    )
```

```python
import jax
import jax.numpy as jnp
from jax import lax
from jax.experimental import pallas as pl
from jax.experimental.pallas import tpu as pltpu
from jax.sharding import PartitionSpec as P

ORDER = 4
NORB = 104
TILES = 11
PER = 5
FAR = (12, 11, 13, 4, 10, 14, 3, 5, 9, 15, 2, 6, 8, 1, 7, 0)
BLOCKS = ((0, 64, (0, 2, 1, 3)), (64, 256, (4, 6, 5, 8, 7, 10, 12, 14, 9, 11, 13, 15)))
MESH = pl.DeviceIdType.MESH
F32, BF16 = jnp.float32, jnp.bfloat16


def place():
    walk, pb = lax.axis_index("walk"), lax.axis_index("pb")
    return walk, pb, walk // 2, lax.rem(walk, 2)


def moved(site, step):
    z = lax.rem(site // 2 + lax.rem(step, 8), 8)
    return z * 2 + lax.rem(lax.rem(site, 2) + step // 8, 2)


def tile_of(site, pb):
    spot = lax.rem(lax.rem(site, 2) * 8 + site // 2 + 2 * (pb // 4) + lax.rem(pb, 4), 16)
    return spot - (spot + 1) // 3, lax.rem(spot, 3) != 1, pb // 8


def lanes_of(shape):
    return lax.broadcasted_iota(jnp.int32, shape, len(shape) - 1)


def unflatten(ref, lead, mats, rows):
    for a in range(13):
        x = (ref[0, :, a * 1664 : (a + 1) * 1664] if lead else ref[:, a * 1664 : (a + 1) * 1664]).astype(F32)
        y = jnp.stack([x[:, 208 * i : 208 * (i + 1)] for i in range(8)], axis=0)
        mats[:, 8 * a : 8 * a + 8, 0:208] = jnp.transpose(y, (1, 0, 2))


def pack(mats, packed):
    lanes = lanes_of((16, 128))
    for g in range(PER):
        for b in range(6):
            packed[b, g] = mats[g, 16 * b : 16 * b + 16, 0:128].astype(BF16)
        tail = jnp.where(lanes[:8] < 64, mats[g, 96:104, 128:256], 0.0)
        packed[6, g] = jnp.concatenate([mats[g, 96:104, 0:128], tail], axis=0).astype(BF16)
        for m in range(3):
            even = mats[g, 32 * m : 32 * m + 16, 128:256]
            odd = mats[g, 32 * m + 16 : 32 * m + 32, 128:256]
            packed[7 + m, g] = jnp.where(lanes < 64, even, pltpu.roll(odd, 64, 1)).astype(BF16)
        last = jnp.zeros((16, 128), F32)
        for b in range(7):
            block = mats[g, 16 * b : 16 * b + 16, 128:256]
            if b == 6:
                block = jnp.where(lax.broadcasted_iota(jnp.int32, (16, 128), 0) < 8, block, 0.0)
            block = pltpu.roll(block, (16 * b - 64) % 128, 1)
            last = jnp.where((lanes >= 16 * b) & (lanes < 16 * b + 16), block, last)
        packed[10, g] = last.astype(BF16)


def unpack(hr, right, j):
    lanes = lanes_of((16, 128))
    last = hr[j * TILES + 10].astype(F32)
    for b in range(7):
        if b < 6:
            block = hr[j * TILES + 7 + b // 2].astype(F32)
            if b % 2:
                block = pltpu.roll(block, 64, 1)
        else:
            block = hr[j * TILES + 6].astype(F32)
            block = jnp.concatenate([block[8:16], jnp.zeros((8, 128), F32)], axis=0)
        end = pltpu.roll(last, (64 - 16 * b) % 128, 1)
        block = jnp.where(lanes < 64, block, jnp.where(lanes < 80, end, 0.0))
        right[j, 16 * b : 16 * b + 16] = block.astype(BF16)
    right[j, 112:128] = jnp.zeros((16, 128), BF16)


def complex_join(acc):
    keep = lanes_of((4, 128)) < NORB
    low, high = acc[:, 0:128], acc[:, NORB : NORB + 128]
    return jnp.where(keep, low[0:4] - high[4:8], 0.0), jnp.where(keep, high[0:4] + low[4:8], 0.0)


def as_rows(rows):
    return jnp.concatenate([rows, jnp.zeros((8, 128), F32)], axis=0).astype(BF16)


def field_tile(fields, charge):
    f = jnp.zeros((8, 160), F32)
    for q in range(4):
        f = jnp.where(charge == q, fields[0, :, q, :], f)
    rest = jnp.concatenate([f[:, 128:160], jnp.zeros((8, 96), F32)], axis=1)
    return jnp.concatenate([f[:, 0:128], rest], axis=0).astype(BF16)


def split_rows(bras, mine, k):
    wide = jnp.concatenate([bras[mine, k].astype(F32), jnp.zeros((4, 48), F32)], axis=1)
    keep = lanes_of((4, 128)) < NORB
    halves = [jnp.where(keep, wide[:, i : i + 128], 0.0) for i in (0, NORB)]
    return jnp.concatenate(halves, axis=0)


def kernel(
    bras_in, fields_in, chol_in, one_body_in, pairs_in, kpq_in, out,
    bras, fields, chol, one_body, pairs, kpq,
    mats, obm, propagator, packed, crecv, cmat, plain, hs, hr, right, current, obuf,
    load, hrec, csend, crec, hsend, osend, orec, ready,
):
    walk, pb, site, core = place()
    tile, makes, maker_core = tile_of(site, pb)
    maker = makes & (maker_core == core)
    active = pb // 8 != core
    mine = lax.rem(pb, 8)

    def remote(src, dst, send, rec, to_walk, to_pb):
        return pltpu.make_async_remote_copy(
            src_ref=src, dst_ref=dst, send_sem=send, recv_sem=rec,
            device_id=(to_walk, to_pb), device_id_type=MESH,
        )

    loads = [
        pltpu.make_async_copy(src, dst, load.at[i])
        for i, (src, dst) in enumerate(
            [(chol_in, chol), (fields_in, fields), (one_body_in, one_body)]
            + [(bras_in, bras), (pairs_in, pairs), (kpq_in, kpq)]
        )
    ]
    barrier = pltpu.get_barrier_semaphore()
    sibling = walk + 1 - 2 * core
    for i in FAR:
        for c in (0, 1) if i else (1,):
            to = moved(site, i) * 2 + lax.rem(core + c, 2)
            pl.semaphore_signal(barrier, inc=1, device_id=(to, pb), device_id_type=MESH)
    for i in range(1, 16):
        pl.semaphore_signal(barrier, inc=1, device_id=(walk, lax.rem(pb + i, 16)), device_id_type=MESH)

    for copy in loads:
        copy.start()
    loads[0].wait()
    unflatten(chol, True, mats, PER)
    pack(mats, packed)
    loads[1].wait()
    loads[4].wait()
    ftile = field_tile(fields, pairs[0, pb])
    for t in range(TILES):
        packed[t, PER] = ftile

    hands = []
    for i in FAR:
        there = moved(site, i)
        t, used, c = tile_of(there, pb)
        hands.append((there, t, used & (c != core) if i == 0 else used, c))
    pl.semaphore_wait(barrier, 46)
    for i in range(1, 16):
        pl.semaphore_signal(ready, inc=1, device_id=(walk, lax.rem(pb + i, 16)), device_id_type=MESH)

    for there, t, used, c in hands:

        @pl.when(used)
        def _():
            remote(packed.at[t], crecv.at[walk], csend, crec, there * 2 + c, pb).start()

    @pl.when(maker)
    def _():
        crecv[walk] = packed[tile]

    loads[2].wait()
    unflatten(one_body, False, obm, 4)
    for k in range(4):
        obm[k, NORB:112] = jnp.zeros((8, 256), F32)
        propagator[k, 0:112] = obm[k].astype(BF16)
        propagator[k, 112:128] = jnp.zeros((16, 256), BF16)
    loads[3].wait()
    loads[5].wait()
    pl.semaphore_wait(ready, 15)

    @pl.when(maker)
    def _():
        remote(crecv.at[0:31], crecv.at[0:31], csend, crec, sibling, pb).wait_recv()
        for kg in range(10):
            block = jnp.stack([crecv[(16 * kg + i) // PER, (16 * kg + i) % PER].astype(F32) for i in range(16)], axis=0)
            cmat[:, 16 * kg : 16 * kg + 16, :] = jnp.transpose(block, (1, 0, 2)).astype(BF16)
        ft = crecv[:, PER].astype(F32)
        f = jnp.concatenate([ft[:, 0:8].reshape(256, 128), ft[:, 8:16].reshape(256, 128)[:, 0:32]], axis=1).astype(BF16)
        def send(to, i):
            return remote(hs.at[to * 8 + i], hr.at[pb * TILES + tile], hsend, hrec.at[pb // 4], to, 8 - lax.rem(to, 2) * 8 + i)

        for start, stop, sites in BLOCKS:
            for p in range(0, 16, 2):
                rhs = jnp.concatenate([cmat[p], cmat[p + 1]], axis=1)
                both = jnp.dot(f[start:stop], rhs, preferred_element_type=F32)
                plain[p, start:stop] = both[:, 0:128]
                plain[p + 1, start:stop] = both[:, 128:256]
            for to in range(start // 8, stop // 8):
                hs[8 * to : 8 * to + 8] = jnp.transpose(plain[:, 8 * to : 8 * to + 8, :], (1, 0, 2)).astype(BF16)
            for there in sites:
                for to in (2 * there, 2 * there + 1):

                    def one(di, carry):
                        send(to, lax.rem(mine + di, 8)).start()
                        return carry

                    lax.fori_loop(0, 8, one, 0)

    @pl.when(active)
    def _():
        sources = [pairs[1, j] for j in range(16)]
        targets = [kpq[pairs[0, j], sources[j]] for j in range(16)]
        summed = [split_rows(bras, mine, k) for k in range(4)]
        for k in range(4):
            current[k] = as_rows(summed[k])

        def arrived(group):
            some = hr.at[pl.ds(group * 4 * TILES, 4 * TILES)]
            return remote(some, some, hsend, hrec.at[group], sibling, pb)

        for n in range(1, ORDER + 1):
            acc = [jnp.zeros((8, 256), F32) for _ in range(4)]
            for j in range(16):
                if n == 1 and j % 4 == 0:
                    arrived(j // 4).wait_recv()
                if n == 1:
                    unpack(hr, right, j)
                matrix = jnp.concatenate([hr[j * TILES : j * TILES + 8].reshape(128, 128), right[j]], axis=1)
                product = jnp.dot(current[sources[j]], matrix, preferred_element_type=F32)[0:8]
                acc = [acc[k] + jnp.where(targets[j] == k, product, 0.0) for k in range(4)]
            for k in range(4):
                scaled = jnp.concatenate(complex_join(acc[k]), axis=0) * (1.0 / n)
                summed[k] = summed[k] + scaled
                current[k] = as_rows(scaled)
        joined = [
            complex_join(jnp.dot(as_rows(summed[k]), propagator[k], preferred_element_type=F32)) for k in range(4)
        ]
        real, imag = (jnp.concatenate([one[i] for one in joined], axis=0) for i in (0, 1))
        zero = jnp.zeros((16, 128), F32)
        wide = jnp.concatenate([real, zero], axis=1)
        wide += pltpu.roll(jnp.concatenate([imag, zero], axis=1), NORB, 1)
        obuf[mine] = wide.astype(BF16)
        for i in range(1, 16):
            remote(obuf.at[mine], obuf.at[mine], osend, orec, walk, lax.rem(pb + i, 16)).start()
        remote(obuf.at[0:7], obuf.at[0:7], osend, orec, sibling, pb).wait_recv()

    @pl.when(jnp.logical_not(active))
    def _():
        remote(obuf, obuf, osend, orec, sibling, pb).wait_recv()

    for w in range(8):
        rows = obuf[w].astype(F32)
        for k in range(4):
            out[w, k] = rows[4 * k : 4 * k + 4, 0 : 2 * NORB].astype(BF16)

    @pl.when(maker)
    def _():
        remote(packed.at[0:10], packed.at[0:10], csend, crec, sibling, pb).wait_send()

        remote(hs, hs, hsend, hrec.at[0], sibling, pb).wait_send()

    @pl.when(jnp.logical_not(maker))
    def _():
        remote(packed, packed, csend, crec, sibling, pb).wait_send()

    @pl.when(active)
    def _():
        remote(hs.at[0:30], hs.at[0:30], osend, orec, sibling, pb).wait_send()


def shards(bras, fields, chol, one_body, pair_table, kpq_map):
    dma = pltpu.SemaphoreType.DMA(())
    return pl.pallas_call(
        kernel,
        out_shape=jax.ShapeDtypeStruct(bras.shape, BF16),
        in_specs=[pl.BlockSpec(memory_space=pltpu.HBM)] * 6,
        out_specs=pl.BlockSpec(memory_space=pltpu.VMEM),
        scratch_shapes=[
            pltpu.VMEM(bras.shape, BF16),
            pltpu.VMEM(fields.shape, F32),
            pltpu.VMEM(chol.shape, BF16),
            pltpu.VMEM(one_body.shape, BF16),
            pltpu.SMEM((2, 16), jnp.int32),
            pltpu.SMEM((4, 4), jnp.int32),
            pltpu.VMEM((PER, 112, 256), F32),
            pltpu.VMEM((4, 112, 256), F32),
            pltpu.VMEM((4, 128, 256), BF16),
            pltpu.VMEM((TILES, PER + 1, 16, 128), BF16),
            pltpu.VMEM((32, PER + 1, 16, 128), BF16),
            pltpu.VMEM((16, 160, 128), BF16),
            pltpu.VMEM((16, 256, 128), F32),
            pltpu.VMEM((256, 16, 128), BF16),
            pltpu.VMEM((16 * TILES, 16, 128), BF16),
            pltpu.VMEM((16, 128, 128), BF16),
            pltpu.VMEM((4, 16, 128), BF16),
            pltpu.VMEM((8, 16, 256), BF16),
            pltpu.SemaphoreType.DMA((6,)),
            pltpu.SemaphoreType.DMA((4,)),
            *[dma] * 5,
            pltpu.SemaphoreType.REGULAR,
        ],
        compiler_params=pltpu.CompilerParams(
            collective_id=0, has_side_effects=True, vmem_limit_bytes=60 * 2**20
        ),
        cost_estimate=pl.CostEstimate(flops=10**8, bytes_accessed=10**6, transcendentals=0),
    )(bras, fields, chol, one_body, pair_table.T, kpq_map)


def solution(mesh):
    return jax.shard_map(
        shards,
        mesh=mesh,
        in_specs=(
            P("walk", None, None, None),
            P(None, "walk", None, None),
            P("pb", "walk", None),
            P(),
            P(),
            P(),
        ),
        out_specs=P("walk", None, None, None),
        check_vma=False,
    )
```

```python
import jax
import jax.numpy as jnp
from jax import lax
from jax.experimental import pallas as pl
from jax.experimental.pallas import tpu as pltpu
from jax.sharding import PartitionSpec as P

ORDER = 4
NORB = 104
TILES = 11
PER = 5
FAR = (12, 11, 13, 4, 10, 14, 3, 5, 9, 15, 2, 6, 8, 1, 7, 0)
BLOCKS = ((0, 64, (0, 2, 1, 3)), (64, 256, (4, 6, 5, 8, 7, 10, 12, 14, 9, 11, 13, 15)))
MESH = pl.DeviceIdType.MESH
F32, BF16 = jnp.float32, jnp.bfloat16


def place():
    walk, pb = lax.axis_index("walk"), lax.axis_index("pb")
    return walk, pb, walk // 2, lax.rem(walk, 2)


def moved(site, step):
    z = lax.rem(site // 2 + lax.rem(step, 8), 8)
    return z * 2 + lax.rem(lax.rem(site, 2) + step // 8, 2)


def tile_of(site, pb):
    spot = lax.rem(lax.rem(site, 2) * 8 + site // 2 + 2 * (pb // 4) + lax.rem(pb, 4), 16)
    return spot - (spot + 1) // 3, lax.rem(spot, 3) != 1, pb // 8


def lanes_of(shape):
    return lax.broadcasted_iota(jnp.int32, shape, len(shape) - 1)


def unflatten(ref, lead, mats, rows):
    for a in range(13):
        x = (ref[0, :, a * 1664 : (a + 1) * 1664] if lead else ref[:, a * 1664 : (a + 1) * 1664]).astype(F32)
        y = jnp.stack([x[:, 208 * i : 208 * (i + 1)] for i in range(8)], axis=0)
        mats[:, 8 * a : 8 * a + 8, 0:208] = jnp.transpose(y, (1, 0, 2))


def pack(mats, packed):
    lanes = lanes_of((16, 128))
    for g in range(PER):
        for b in range(6):
            packed[b, g] = mats[g, 16 * b : 16 * b + 16, 0:128].astype(BF16)
        tail = jnp.where(lanes[:8] < 64, mats[g, 96:104, 128:256], 0.0)
        packed[6, g] = jnp.concatenate([mats[g, 96:104, 0:128], tail], axis=0).astype(BF16)
        for m in range(3):
            even = mats[g, 32 * m : 32 * m + 16, 128:256]
            odd = mats[g, 32 * m + 16 : 32 * m + 32, 128:256]
            packed[7 + m, g] = jnp.where(lanes < 64, even, pltpu.roll(odd, 64, 1)).astype(BF16)
        last = jnp.zeros((16, 128), F32)
        for b in range(7):
            block = mats[g, 16 * b : 16 * b + 16, 128:256]
            if b == 6:
                block = jnp.where(lax.broadcasted_iota(jnp.int32, (16, 128), 0) < 8, block, 0.0)
            block = pltpu.roll(block, (16 * b - 64) % 128, 1)
            last = jnp.where((lanes >= 16 * b) & (lanes < 16 * b + 16), block, last)
        packed[10, g] = last.astype(BF16)


def unpack(hr, right, j):
    lanes = lanes_of((16, 128))
    last = hr[j * TILES + 10].astype(F32)
    for b in range(7):
        if b < 6:
            block = hr[j * TILES + 7 + b // 2].astype(F32)
            if b % 2:
                block = pltpu.roll(block, 64, 1)
        else:
            block = hr[j * TILES + 6].astype(F32)
            block = jnp.concatenate([block[8:16], jnp.zeros((8, 128), F32)], axis=0)
        end = pltpu.roll(last, (64 - 16 * b) % 128, 1)
        block = jnp.where(lanes < 64, block, jnp.where(lanes < 80, end, 0.0))
        right[j, 16 * b : 16 * b + 16] = block.astype(BF16)
    right[j, 112:128] = jnp.zeros((16, 128), BF16)


def complex_join(acc):
    keep = lanes_of((4, 128)) < NORB
    low, high = acc[:, 0:128], acc[:, NORB : NORB + 128]
    return jnp.where(keep, low[0:4] - high[4:8], 0.0), jnp.where(keep, high[0:4] + low[4:8], 0.0)


def as_rows(rows):
    return jnp.concatenate([rows, jnp.zeros((8, 128), F32)], axis=0).astype(BF16)


def field_tile(fields, charge):
    f = jnp.zeros((8, 160), F32)
    for q in range(4):
        f = jnp.where(charge == q, fields[0, :, q, :], f)
    rest = jnp.concatenate([f[:, 128:160], jnp.zeros((8, 96), F32)], axis=1)
    return jnp.concatenate([f[:, 0:128], rest], axis=0).astype(BF16)


def split_rows(bras, mine, k):
    wide = jnp.concatenate([bras[mine, k].astype(F32), jnp.zeros((4, 48), F32)], axis=1)
    keep = lanes_of((4, 128)) < NORB
    halves = [jnp.where(keep, wide[:, i : i + 128], 0.0) for i in (0, NORB)]
    return jnp.concatenate(halves, axis=0)


def kernel(
    bras_in, fields_in, chol_in, one_body_in, pairs_in, kpq_in, out,
    bras, fields, chol, one_body, pairs, kpq,
    mats, obm, propagator, packed, crecv, cmat, plain, hs, hr, right, current, obuf,
    load, hrec, csend, crec, hsend, osend, orec, ready,
):
    walk, pb, site, core = place()
    tile, makes, maker_core = tile_of(site, pb)
    maker = makes & (maker_core == core)
    active = pb // 8 != core
    mine = lax.rem(pb, 8)

    def remote(src, dst, send, rec, to_walk, to_pb):
        return pltpu.make_async_remote_copy(
            src_ref=src, dst_ref=dst, send_sem=send, recv_sem=rec,
            device_id=(to_walk, to_pb), device_id_type=MESH,
        )

    loads = [
        pltpu.make_async_copy(src, dst, load.at[i])
        for i, (src, dst) in enumerate(
            [(chol_in, chol), (fields_in, fields), (one_body_in, one_body)]
            + [(bras_in, bras), (pairs_in, pairs), (kpq_in, kpq)]
        )
    ]
    barrier = pltpu.get_barrier_semaphore()
    sibling = walk + 1 - 2 * core
    for i in FAR:
        for c in (0, 1) if i else (1,):
            to = moved(site, i) * 2 + lax.rem(core + c, 2)
            pl.semaphore_signal(barrier, inc=1, device_id=(to, pb), device_id_type=MESH)
    for i in range(1, 16):
        pl.semaphore_signal(barrier, inc=1, device_id=(walk, lax.rem(pb + i, 16)), device_id_type=MESH)

    for copy in loads:
        copy.start()
    loads[0].wait()
    unflatten(chol, True, mats, PER)
    pack(mats, packed)
    loads[1].wait()
    loads[4].wait()
    ftile = field_tile(fields, pairs[0, pb])
    for t in range(TILES):
        packed[t, PER] = ftile

    hands = []
    for i in FAR:
        there = moved(site, i)
        t, used, c = tile_of(there, pb)
        hands.append((there, t, used & (c != core) if i == 0 else used, c))
    pl.semaphore_wait(barrier, 46)
    for i in range(1, 16):
        pl.semaphore_signal(ready, inc=1, device_id=(walk, lax.rem(pb + i, 16)), device_id_type=MESH)

    for there, t, used, c in hands:

        @pl.when(used)
        def _():
            remote(packed.at[t], crecv.at[walk], csend, crec, there * 2 + c, pb).start()

    @pl.when(maker)
    def _():
        crecv[walk] = packed[tile]

    loads[2].wait()
    unflatten(one_body, False, obm, 4)
    for k in range(4):
        obm[k, NORB:112] = jnp.zeros((8, 256), F32)
        propagator[k, 0:112] = obm[k].astype(BF16)
        propagator[k, 112:128] = jnp.zeros((16, 256), BF16)
    loads[3].wait()
    loads[5].wait()
    pl.semaphore_wait(ready, 15)

    @pl.when(maker)
    def _():
        remote(crecv.at[0:31], crecv.at[0:31], csend, crec, sibling, pb).wait_recv()
        for kg in range(10):
            block = jnp.stack([crecv[(16 * kg + i) // PER, (16 * kg + i) % PER].astype(F32) for i in range(16)], axis=0)
            cmat[:, 16 * kg : 16 * kg + 16, :] = jnp.transpose(block, (1, 0, 2)).astype(BF16)
        ft = crecv[:, PER].astype(F32)
        f = jnp.concatenate([ft[:, 0:8].reshape(256, 128), ft[:, 8:16].reshape(256, 128)[:, 0:32]], axis=1).astype(BF16)
        def send(to, i):
            return remote(hs.at[to * 8 + i], hr.at[pb * TILES + tile], hsend, hrec.at[pb // 4], to, 8 - lax.rem(to, 2) * 8 + i)

        for start, stop, sites in BLOCKS:
            for p in range(0, 16, 2):
                rhs = jnp.concatenate([cmat[p], cmat[p + 1]], axis=1)
                both = jnp.dot(f[start:stop], rhs, preferred_element_type=F32)
                plain[p, start:stop] = both[:, 0:128]
                plain[p + 1, start:stop] = both[:, 128:256]
            for to in range(start // 8, stop // 8):
                hs[8 * to : 8 * to + 8] = jnp.transpose(plain[:, 8 * to : 8 * to + 8, :], (1, 0, 2)).astype(BF16)
            for there in sites:
                for to in (2 * there, 2 * there + 1):

                    def one(di, carry):
                        send(to, lax.rem(mine + di, 8)).start()
                        return carry

                    lax.fori_loop(0, 8, one, 0)

    @pl.when(active)
    def _():
        sources = [pairs[1, j] for j in range(16)]
        targets = [kpq[pairs[0, j], sources[j]] for j in range(16)]
        summed = [split_rows(bras, mine, k) for k in range(4)]
        for k in range(4):
            current[k] = as_rows(summed[k])

        def arrived(group):
            some = hr.at[pl.ds(group * 4 * TILES, 4 * TILES)]
            return remote(some, some, hsend, hrec.at[group], sibling, pb)

        for n in range(1, ORDER + 1):
            acc = [jnp.zeros((8, 256), F32) for _ in range(4)]
            for j in range(16):
                if n == 1 and j % 4 == 0:
                    arrived(j // 4).wait_recv()
                if n == 1:
                    unpack(hr, right, j)
                matrix = jnp.concatenate([hr[j * TILES : j * TILES + 8].reshape(128, 128), right[j]], axis=1)
                product = jnp.dot(current[sources[j]], matrix, preferred_element_type=F32)[0:8]
                acc = [acc[k] + jnp.where(targets[j] == k, product, 0.0) for k in range(4)]
            for k in range(4):
                scaled = jnp.concatenate(complex_join(acc[k]), axis=0) * (1.0 / n)
                summed[k] = summed[k] + scaled
                current[k] = as_rows(scaled)
        joined = [
            complex_join(jnp.dot(as_rows(summed[k]), propagator[k], preferred_element_type=F32)) for k in range(4)
        ]
        real, imag = (jnp.concatenate([one[i] for one in joined], axis=0) for i in (0, 1))
        zero = jnp.zeros((16, 128), F32)
        wide = jnp.concatenate([real, zero], axis=1)
        wide += pltpu.roll(jnp.concatenate([imag, zero], axis=1), NORB, 1)
        obuf[mine] = wide.astype(BF16)
        for i in range(1, 16):
            remote(obuf.at[mine], obuf.at[mine], osend, orec, walk, lax.rem(pb + i, 16)).start()
        remote(obuf.at[0:7], obuf.at[0:7], osend, orec, sibling, pb).wait_recv()

    @pl.when(jnp.logical_not(active))
    def _():
        remote(obuf, obuf, osend, orec, sibling, pb).wait_recv()

    for w in range(8):
        rows = obuf[w].astype(F32)
        for k in range(4):
            out[w, k] = rows[4 * k : 4 * k + 4, 0 : 2 * NORB].astype(BF16)

    @pl.when(maker)
    def _():
        remote(packed.at[0:10], packed.at[0:10], csend, crec, sibling, pb).wait_send()

        remote(hs, hs, hsend, hrec.at[0], sibling, pb).wait_send()

    @pl.when(jnp.logical_not(maker))
    def _():
        remote(packed, packed, csend, crec, sibling, pb).wait_send()

    @pl.when(active)
    def _():
        remote(hs.at[0:30], hs.at[0:30], osend, orec, sibling, pb).wait_send()


def shards(bras, fields, chol, one_body, pair_table, kpq_map):
    dma = pltpu.SemaphoreType.DMA(())
    return pl.pallas_call(
        kernel,
        out_shape=pltpu.VMEM(bras.shape, BF16),
        in_specs=[pl.BlockSpec(memory_space=pltpu.HBM)] * 6,
        out_specs=pl.BlockSpec(memory_space=pltpu.VMEM),
        scratch_shapes=[
            pltpu.VMEM(bras.shape, BF16),
            pltpu.VMEM(fields.shape, F32),
            pltpu.VMEM(chol.shape, BF16),
            pltpu.VMEM(one_body.shape, BF16),
            pltpu.SMEM((2, 16), jnp.int32),
            pltpu.SMEM((4, 4), jnp.int32),
            pltpu.VMEM((PER, 112, 256), F32),
            pltpu.VMEM((4, 112, 256), F32),
            pltpu.VMEM((4, 128, 256), BF16),
            pltpu.VMEM((TILES, PER + 1, 16, 128), BF16),
            pltpu.VMEM((32, PER + 1, 16, 128), BF16),
            pltpu.VMEM((16, 160, 128), BF16),
            pltpu.VMEM((16, 256, 128), F32),
            pltpu.VMEM((256, 16, 128), BF16),
            pltpu.VMEM((16 * TILES, 16, 128), BF16),
            pltpu.VMEM((16, 128, 128), BF16),
            pltpu.VMEM((4, 16, 128), BF16),
            pltpu.VMEM((8, 16, 256), BF16),
            pltpu.SemaphoreType.DMA((6,)),
            pltpu.SemaphoreType.DMA((4,)),
            *[dma] * 5,
            pltpu.SemaphoreType.REGULAR,
        ],
        compiler_params=pltpu.CompilerParams(
            collective_id=0, has_side_effects=True, vmem_limit_bytes=60 * 2**20
        ),
        cost_estimate=pl.CostEstimate(flops=10**8, bytes_accessed=10**6, transcendentals=0),
    )(bras, fields, chol, one_body, pair_table.T, kpq_map)


def solution(mesh):
    return jax.shard_map(
        shards,
        mesh=mesh,
        in_specs=(
            P("walk", None, None, None),
            P(None, "walk", None, None),
            P("pb", "walk", None),
            P(),
            P(),
            P(),
        ),
        out_specs=P("walk", None, None, None),
        check_vma=False,
    )
```

```python
import jax
import jax.numpy as jnp
from jax import lax
from jax.experimental import pallas as pl
from jax.experimental.pallas import tpu as pltpu
from jax.sharding import PartitionSpec as P

ORDER = 4
NORB = 104
TILES = 11
PER = 5
FAR = (12, 11, 13, 4, 10, 14, 3, 5, 9, 15, 2, 6, 8, 1, 7, 0)
BLOCKS = ((0, 32, (0, 1)), (32, 256, (2, 3, 4, 6, 5, 8, 7, 10, 12, 14, 9, 11, 13, 15)))
MESH = pl.DeviceIdType.MESH
F32, BF16 = jnp.float32, jnp.bfloat16


def place():
    walk, pb = lax.axis_index("walk"), lax.axis_index("pb")
    return walk, pb, walk // 2, lax.rem(walk, 2)


def moved(site, step):
    z = lax.rem(site // 2 + lax.rem(step, 8), 8)
    return z * 2 + lax.rem(lax.rem(site, 2) + step // 8, 2)


def tile_of(site, pb):
    spot = lax.rem(lax.rem(site, 2) * 8 + site // 2 + 2 * (pb // 4) + lax.rem(pb, 4), 16)
    return spot - (spot + 1) // 3, lax.rem(spot, 3) != 1, pb // 8


def lanes_of(shape):
    return lax.broadcasted_iota(jnp.int32, shape, len(shape) - 1)


def unflatten(ref, lead, mats, rows):
    for a in range(13):
        x = (ref[0, :, a * 1664 : (a + 1) * 1664] if lead else ref[:, a * 1664 : (a + 1) * 1664]).astype(F32)
        y = jnp.stack([x[:, 208 * i : 208 * (i + 1)] for i in range(8)], axis=0)
        mats[:, 8 * a : 8 * a + 8, 0:208] = jnp.transpose(y, (1, 0, 2))


def pack(mats, packed):
    lanes = lanes_of((16, 128))
    for g in range(PER):
        for b in range(6):
            packed[b, g] = mats[g, 16 * b : 16 * b + 16, 0:128].astype(BF16)
        tail = jnp.where(lanes[:8] < 64, mats[g, 96:104, 128:256], 0.0)
        packed[6, g] = jnp.concatenate([mats[g, 96:104, 0:128], tail], axis=0).astype(BF16)
        for m in range(3):
            even = mats[g, 32 * m : 32 * m + 16, 128:256]
            odd = mats[g, 32 * m + 16 : 32 * m + 32, 128:256]
            packed[7 + m, g] = jnp.where(lanes < 64, even, pltpu.roll(odd, 64, 1)).astype(BF16)
        last = jnp.zeros((16, 128), F32)
        for b in range(7):
            block = mats[g, 16 * b : 16 * b + 16, 128:256]
            if b == 6:
                block = jnp.where(lax.broadcasted_iota(jnp.int32, (16, 128), 0) < 8, block, 0.0)
            block = pltpu.roll(block, (16 * b - 64) % 128, 1)
            last = jnp.where((lanes >= 16 * b) & (lanes < 16 * b + 16), block, last)
        packed[10, g] = last.astype(BF16)


def unpack(hr, right, j):
    lanes = lanes_of((16, 128))
    last = hr[j * TILES + 10].astype(F32)
    for b in range(7):
        if b < 6:
            block = hr[j * TILES + 7 + b // 2].astype(F32)
            if b % 2:
                block = pltpu.roll(block, 64, 1)
        else:
            block = hr[j * TILES + 6].astype(F32)
            block = jnp.concatenate([block[8:16], jnp.zeros((8, 128), F32)], axis=0)
        end = pltpu.roll(last, (64 - 16 * b) % 128, 1)
        block = jnp.where(lanes < 64, block, jnp.where(lanes < 80, end, 0.0))
        right[j, 16 * b : 16 * b + 16] = block.astype(BF16)
    right[j, 112:128] = jnp.zeros((16, 128), BF16)


def complex_join(acc):
    keep = lanes_of((4, 128)) < NORB
    low, high = acc[:, 0:128], acc[:, NORB : NORB + 128]
    return jnp.where(keep, low[0:4] - high[4:8], 0.0), jnp.where(keep, high[0:4] + low[4:8], 0.0)


def as_rows(rows):
    return jnp.concatenate([rows, jnp.zeros((8, 128), F32)], axis=0).astype(BF16)


def field_tile(fields, charge):
    f = jnp.zeros((8, 160), F32)
    for q in range(4):
        f = jnp.where(charge == q, fields[0, :, q, :], f)
    rest = jnp.concatenate([f[:, 128:160], jnp.zeros((8, 96), F32)], axis=1)
    return jnp.concatenate([f[:, 0:128], rest], axis=0).astype(BF16)


def split_rows(bras, mine, k):
    wide = jnp.concatenate([bras[mine, k].astype(F32), jnp.zeros((4, 48), F32)], axis=1)
    keep = lanes_of((4, 128)) < NORB
    halves = [jnp.where(keep, wide[:, i : i + 128], 0.0) for i in (0, NORB)]
    return jnp.concatenate(halves, axis=0)


def kernel(
    bras_in, fields_in, chol_in, one_body_in, pairs_in, kpq_in, out,
    bras, fields, chol, one_body, pairs, kpq,
    mats, obm, propagator, packed, crecv, cmat, plain, hs, hr, right, current, obuf,
    load, hrec, csend, crec, hsend, osend, orec, ready,
):
    walk, pb, site, core = place()
    tile, makes, maker_core = tile_of(site, pb)
    maker = makes & (maker_core == core)
    active = pb // 8 != core
    mine = lax.rem(pb, 8)

    def remote(src, dst, send, rec, to_walk, to_pb):
        return pltpu.make_async_remote_copy(
            src_ref=src, dst_ref=dst, send_sem=send, recv_sem=rec,
            device_id=(to_walk, to_pb), device_id_type=MESH,
        )

    loads = [
        pltpu.make_async_copy(src, dst, load.at[i])
        for i, (src, dst) in enumerate(
            [(chol_in, chol), (fields_in, fields), (one_body_in, one_body)]
            + [(bras_in, bras), (pairs_in, pairs), (kpq_in, kpq)]
        )
    ]
    barrier = pltpu.get_barrier_semaphore()
    sibling = walk + 1 - 2 * core
    for i in FAR:
        for c in (0, 1) if i else (1,):
            to = moved(site, i) * 2 + lax.rem(core + c, 2)
            pl.semaphore_signal(barrier, inc=1, device_id=(to, pb), device_id_type=MESH)
    for i in range(1, 16):
        pl.semaphore_signal(barrier, inc=1, device_id=(walk, lax.rem(pb + i, 16)), device_id_type=MESH)

    for copy in loads:
        copy.start()
    loads[0].wait()
    unflatten(chol, True, mats, PER)
    pack(mats, packed)
    loads[1].wait()
    loads[4].wait()
    ftile = field_tile(fields, pairs[0, pb])
    for t in range(TILES):
        packed[t, PER] = ftile

    hands = []
    for i in FAR:
        there = moved(site, i)
        t, used, c = tile_of(there, pb)
        hands.append((there, t, used & (c != core) if i == 0 else used, c))
    pl.semaphore_wait(barrier, 46)
    for i in range(1, 16):
        pl.semaphore_signal(ready, inc=1, device_id=(walk, lax.rem(pb + i, 16)), device_id_type=MESH)

    for there, t, used, c in hands:

        @pl.when(used)
        def _():
            remote(packed.at[t], crecv.at[walk], csend, crec.at[walk // 16], there * 2 + c, pb).start()

    @pl.when(maker)
    def _():
        crecv[walk] = packed[tile]

    loads[2].wait()
    unflatten(one_body, False, obm, 4)
    for k in range(4):
        obm[k, NORB:112] = jnp.zeros((8, 256), F32)
        propagator[k, 0:112] = obm[k].astype(BF16)
        propagator[k, 112:128] = jnp.zeros((16, 256), BF16)
    loads[3].wait()
    loads[5].wait()
    pl.semaphore_wait(ready, 15)

    @pl.when(maker)
    def _():
        for half in range(2):

            @pl.when(walk // 16 == half)
            def _():
                remote(crecv.at[0:15], crecv.at[0:15], csend, crec.at[half], sibling, pb).wait_recv()

            @pl.when(walk // 16 != half)
            def _():
                remote(crecv.at[0:16], crecv.at[0:16], csend, crec.at[half], sibling, pb).wait_recv()

            for kg in range(5 * half, 5 * half + 5):
                rows = [(16 * kg + i) // PER for i in range(16)]
                block = jnp.stack([crecv[r, (16 * kg + i) % PER].astype(F32) for i, r in enumerate(rows)], axis=0)
                cmat[:, 16 * kg : 16 * kg + 16, :] = jnp.transpose(block, (1, 0, 2)).astype(BF16)
        ft = crecv[:, PER].astype(F32)
        f = jnp.concatenate([ft[:, 0:8].reshape(256, 128), ft[:, 8:16].reshape(256, 128)[:, 0:32]], axis=1).astype(BF16)
        def send(to, i):
            return remote(hs.at[to * 8 + i], hr.at[pb * TILES + tile], hsend, hrec.at[pb // 4], to, 8 - lax.rem(to, 2) * 8 + i)

        for start, stop, sites in BLOCKS:
            for p in range(0, 16, 2):
                rhs = jnp.concatenate([cmat[p], cmat[p + 1]], axis=1)
                both = jnp.dot(f[start:stop], rhs, preferred_element_type=F32)
                plain[p, start:stop] = both[:, 0:128]
                plain[p + 1, start:stop] = both[:, 128:256]
            for to in range(start // 8, stop // 8):
                hs[8 * to : 8 * to + 8] = jnp.transpose(plain[:, 8 * to : 8 * to + 8, :], (1, 0, 2)).astype(BF16)
            for there in sites:
                for to in (2 * there, 2 * there + 1):

                    def one(di, carry):
                        send(to, lax.rem(mine + di, 8)).start()
                        return carry

                    lax.fori_loop(0, 8, one, 0)

    @pl.when(active)
    def _():
        sources = [pairs[1, j] for j in range(16)]
        targets = [kpq[pairs[0, j], sources[j]] for j in range(16)]
        summed = [split_rows(bras, mine, k) for k in range(4)]
        for k in range(4):
            current[k] = as_rows(summed[k])

        def arrived(group):
            some = hr.at[pl.ds(group * 4 * TILES, 4 * TILES)]
            return remote(some, some, hsend, hrec.at[group], sibling, pb)

        for n in range(1, ORDER + 1):
            acc = [jnp.zeros((8, 256), F32) for _ in range(4)]
            for j in range(16):
                if n == 1 and j % 4 == 0:
                    arrived(j // 4).wait_recv()
                if n == 1:
                    unpack(hr, right, j)
                matrix = jnp.concatenate([hr[j * TILES : j * TILES + 8].reshape(128, 128), right[j]], axis=1)
                product = jnp.dot(current[sources[j]], matrix, preferred_element_type=F32)[0:8]
                acc = [acc[k] + jnp.where(targets[j] == k, product, 0.0) for k in range(4)]
            for k in range(4):
                scaled = jnp.concatenate(complex_join(acc[k]), axis=0) * (1.0 / n)
                summed[k] = summed[k] + scaled
                current[k] = as_rows(scaled)
        joined = [
            complex_join(jnp.dot(as_rows(summed[k]), propagator[k], preferred_element_type=F32)) for k in range(4)
        ]
        real, imag = (jnp.concatenate([one[i] for one in joined], axis=0) for i in (0, 1))
        zero = jnp.zeros((16, 128), F32)
        wide = jnp.concatenate([real, zero], axis=1)
        wide += pltpu.roll(jnp.concatenate([imag, zero], axis=1), NORB, 1)
        obuf[mine] = wide.astype(BF16)
        for i in range(1, 16):
            remote(obuf.at[mine], obuf.at[mine], osend, orec, walk, lax.rem(pb + i, 16)).start()
        remote(obuf.at[0:7], obuf.at[0:7], osend, orec, sibling, pb).wait_recv()

    @pl.when(jnp.logical_not(active))
    def _():
        remote(obuf, obuf, osend, orec, sibling, pb).wait_recv()

    for w in range(8):
        rows = obuf[w].astype(F32)
        for k in range(4):
            out[w, k] = rows[4 * k : 4 * k + 4, 0 : 2 * NORB].astype(BF16)

    @pl.when(maker)
    def _():
        remote(packed.at[0:10], packed.at[0:10], csend, crec.at[0], sibling, pb).wait_send()

        remote(hs, hs, hsend, hrec.at[0], sibling, pb).wait_send()

    @pl.when(jnp.logical_not(maker))
    def _():
        remote(packed, packed, csend, crec.at[0], sibling, pb).wait_send()

    @pl.when(active)
    def _():
        remote(hs.at[0:30], hs.at[0:30], osend, orec, sibling, pb).wait_send()


def shards(bras, fields, chol, one_body, pair_table, kpq_map):
    dma = pltpu.SemaphoreType.DMA(())
    return pl.pallas_call(
        kernel,
        out_shape=pltpu.VMEM(bras.shape, BF16),
        in_specs=[pl.BlockSpec(memory_space=pltpu.HBM)] * 6,
        out_specs=pl.BlockSpec(memory_space=pltpu.VMEM),
        scratch_shapes=[
            pltpu.VMEM(bras.shape, BF16),
            pltpu.VMEM(fields.shape, F32),
            pltpu.VMEM(chol.shape, BF16),
            pltpu.VMEM(one_body.shape, BF16),
            pltpu.SMEM((2, 16), jnp.int32),
            pltpu.SMEM((4, 4), jnp.int32),
            pltpu.VMEM((PER, 112, 256), F32),
            pltpu.VMEM((4, 112, 256), F32),
            pltpu.VMEM((4, 128, 256), BF16),
            pltpu.VMEM((TILES, PER + 1, 16, 128), BF16),
            pltpu.VMEM((32, PER + 1, 16, 128), BF16),
            pltpu.VMEM((16, 160, 128), BF16),
            pltpu.VMEM((16, 256, 128), F32),
            pltpu.VMEM((256, 16, 128), BF16),
            pltpu.VMEM((16 * TILES, 16, 128), BF16),
            pltpu.VMEM((16, 128, 128), BF16),
            pltpu.VMEM((4, 16, 128), BF16),
            pltpu.VMEM((8, 16, 256), BF16),
            pltpu.SemaphoreType.DMA((6,)),
            pltpu.SemaphoreType.DMA((4,)),
            dma,
            pltpu.SemaphoreType.DMA((2,)),
            *[dma] * 3,
            pltpu.SemaphoreType.REGULAR,
        ],
        compiler_params=pltpu.CompilerParams(
            collective_id=0, has_side_effects=True, vmem_limit_bytes=60 * 2**20
        ),
        cost_estimate=pl.CostEstimate(flops=10**8, bytes_accessed=10**6, transcendentals=0),
    )(bras, fields, chol, one_body, pair_table.T, kpq_map)


def solution(mesh):
    return jax.shard_map(
        shards,
        mesh=mesh,
        in_specs=(
            P("walk", None, None, None),
            P(None, "walk", None, None),
            P("pb", "walk", None),
            P(),
            P(),
            P(),
        ),
        out_specs=P("walk", None, None, None),
        check_vma=False,
    )
```

```python
import jax
import jax.numpy as jnp
from jax import lax
from jax.experimental import pallas as pl
from jax.experimental.pallas import tpu as pltpu
from jax.sharding import PartitionSpec as P

ORDER = 4
NORB = 104
TILES = 11
PER = 5
FAR = (12, 11, 13, 4, 10, 14, 3, 5, 9, 15, 2, 6, 8, 1, 7, 0)
BLOCKS = ((0, 32, (0, 1)), (32, 256, (2, 3, 4, 6, 5, 8, 7, 10, 12, 14, 9, 11, 13, 15)))
MESH = pl.DeviceIdType.MESH
F32, BF16 = jnp.float32, jnp.bfloat16


def place():
    walk, pb = lax.axis_index("walk"), lax.axis_index("pb")
    return walk, pb, walk // 2, lax.rem(walk, 2)


def moved(site, step):
    z = lax.rem(site // 2 + lax.rem(step, 8), 8)
    return z * 2 + lax.rem(lax.rem(site, 2) + step // 8, 2)


def tile_of(site, pb):
    spot = lax.rem(lax.rem(site, 2) * 8 + site // 2 + 2 * (pb // 4) + lax.rem(pb, 4), 16)
    return spot - (spot + 1) // 3, lax.rem(spot, 3) != 1, pb // 8


def lanes_of(shape):
    return lax.broadcasted_iota(jnp.int32, shape, len(shape) - 1)


def unflatten(ref, lead, mats, rows):
    for a in range(13):
        x = (ref[0, :, a * 1664 : (a + 1) * 1664] if lead else ref[:, a * 1664 : (a + 1) * 1664]).astype(F32)
        y = jnp.stack([x[:, 208 * i : 208 * (i + 1)] for i in range(8)], axis=0)
        mats[:, 8 * a : 8 * a + 8, 0:208] = jnp.transpose(y, (1, 0, 2))


def pack(mats, packed):
    lanes = lanes_of((16, 128))
    for g in range(PER):
        for b in range(6):
            packed[b, g] = mats[g, 16 * b : 16 * b + 16, 0:128].astype(BF16)
        tail = jnp.where(lanes[:8] < 64, mats[g, 96:104, 128:256], 0.0)
        packed[6, g] = jnp.concatenate([mats[g, 96:104, 0:128], tail], axis=0).astype(BF16)
        for m in range(3):
            even = mats[g, 32 * m : 32 * m + 16, 128:256]
            odd = mats[g, 32 * m + 16 : 32 * m + 32, 128:256]
            packed[7 + m, g] = jnp.where(lanes < 64, even, pltpu.roll(odd, 64, 1)).astype(BF16)
        last = jnp.zeros((16, 128), F32)
        for b in range(7):
            block = mats[g, 16 * b : 16 * b + 16, 128:256]
            if b == 6:
                block = jnp.where(lax.broadcasted_iota(jnp.int32, (16, 128), 0) < 8, block, 0.0)
            block = pltpu.roll(block, (16 * b - 64) % 128, 1)
            last = jnp.where((lanes >= 16 * b) & (lanes < 16 * b + 16), block, last)
        packed[10, g] = last.astype(BF16)


def unpack(hr, right, j):
    lanes = lanes_of((16, 128))
    last = hr[j * TILES + 10].astype(F32)
    for b in range(7):
        if b < 6:
            block = hr[j * TILES + 7 + b // 2].astype(F32)
            if b % 2:
                block = pltpu.roll(block, 64, 1)
        else:
            block = hr[j * TILES + 6].astype(F32)
            block = jnp.concatenate([block[8:16], jnp.zeros((8, 128), F32)], axis=0)
        end = pltpu.roll(last, (64 - 16 * b) % 128, 1)
        block = jnp.where(lanes < 64, block, jnp.where(lanes < 80, end, 0.0))
        right[j, 16 * b : 16 * b + 16] = block.astype(BF16)
    right[j, 112:128] = jnp.zeros((16, 128), BF16)


def complex_join(acc):
    keep = lanes_of((4, 128)) < NORB
    low, high = acc[:, 0:128], acc[:, NORB : NORB + 128]
    return jnp.where(keep, low[0:4] - high[4:8], 0.0), jnp.where(keep, high[0:4] + low[4:8], 0.0)


def as_rows(rows):
    return jnp.concatenate([rows, jnp.zeros((8, 128), F32)], axis=0).astype(BF16)


def field_tile(fields, charge):
    f = jnp.zeros((8, 160), F32)
    for q in range(4):
        f = jnp.where(charge == q, fields[0, :, q, :], f)
    rest = jnp.concatenate([f[:, 128:160], jnp.zeros((8, 96), F32)], axis=1)
    return jnp.concatenate([f[:, 0:128], rest], axis=0).astype(BF16)


def split_rows(bras, mine, k):
    wide = jnp.concatenate([bras[mine, k].astype(F32), jnp.zeros((4, 48), F32)], axis=1)
    keep = lanes_of((4, 128)) < NORB
    halves = [jnp.where(keep, wide[:, i : i + 128], 0.0) for i in (0, NORB)]
    return jnp.concatenate(halves, axis=0)


def kernel(
    bras_in, fields_in, chol_in, one_body_in, pairs_in, kpq_in, out,
    bras, fields, chol, one_body, pairs, kpq,
    mats, obm, propagator, packed, crecv, cmat, plain, hs, hr, right, current, obuf,
    load, hrec, csend, crec, hsend, osend, orec, ready,
):
    walk, pb, site, core = place()
    tile, makes, maker_core = tile_of(site, pb)
    maker = makes & (maker_core == core)
    active = pb // 8 != core
    mine = lax.rem(pb, 8)

    def remote(src, dst, send, rec, to_walk, to_pb):
        return pltpu.make_async_remote_copy(
            src_ref=src, dst_ref=dst, send_sem=send, recv_sem=rec,
            device_id=(to_walk, to_pb), device_id_type=MESH,
        )

    loads = [
        pltpu.make_async_copy(src, dst, load.at[i])
        for i, (src, dst) in enumerate(
            [(chol_in, chol), (fields_in, fields), (one_body_in, one_body)]
            + [(bras_in, bras), (pairs_in, pairs), (kpq_in, kpq)]
        )
    ]
    barrier = pltpu.get_barrier_semaphore()
    sibling = walk + 1 - 2 * core
    for i in FAR:
        for c in (0, 1) if i else (1,):
            to = moved(site, i) * 2 + lax.rem(core + c, 2)
            pl.semaphore_signal(barrier, inc=1, device_id=(to, pb), device_id_type=MESH)
    for i in range(1, 16):
        pl.semaphore_signal(barrier, inc=1, device_id=(walk, lax.rem(pb + i, 16)), device_id_type=MESH)

    for copy in loads:
        copy.start()
    loads[0].wait()
    unflatten(chol, True, mats, PER)
    pack(mats, packed)
    loads[1].wait()
    loads[4].wait()
    ftile = field_tile(fields, pairs[0, pb])
    for t in range(TILES):
        packed[t, PER] = ftile

    hands = []
    for i in FAR:
        there = moved(site, i)
        t, used, c = tile_of(there, pb)
        hands.append((there, t, used & (c != core) if i == 0 else used, c))
    pl.semaphore_wait(barrier, 46)
    for i in range(1, 16):
        pl.semaphore_signal(ready, inc=1, device_id=(walk, lax.rem(pb + i, 16)), device_id_type=MESH)

    for there, t, used, c in hands:

        @pl.when(used)
        def _():
            remote(packed.at[t], crecv.at[walk], csend, crec.at[walk // 16], there * 2 + c, pb).start()

    @pl.when(maker)
    def _():
        crecv[walk] = packed[tile]

    loads[2].wait()
    unflatten(one_body, False, obm, 4)
    for k in range(4):
        obm[k, NORB:112] = jnp.zeros((8, 256), F32)
        propagator[k, 0:112] = obm[k].astype(BF16)
        propagator[k, 112:128] = jnp.zeros((16, 256), BF16)
    loads[3].wait()
    loads[5].wait()
    pl.semaphore_wait(ready, 15)

    @pl.when(maker)
    def _():
        for half in range(2):

            @pl.when(walk // 16 == half)
            def _():
                remote(crecv.at[0:15], crecv.at[0:15], csend, crec.at[half], sibling, pb).wait_recv()

            @pl.when(walk // 16 != half)
            def _():
                remote(crecv.at[0:16], crecv.at[0:16], csend, crec.at[half], sibling, pb).wait_recv()

            for kg in range(5 * half, 5 * half + 5):
                rows = [(16 * kg + i) // PER for i in range(16)]
                block = jnp.stack([crecv[r, (16 * kg + i) % PER].astype(F32) for i, r in enumerate(rows)], axis=0)
                cmat[:, 16 * kg : 16 * kg + 16, :] = jnp.transpose(block, (1, 0, 2)).astype(BF16)
        ft = crecv[:, PER].astype(F32)
        f = jnp.concatenate([ft[:, 0:8].reshape(256, 128), ft[:, 8:16].reshape(256, 128)[:, 0:32]], axis=1).astype(BF16)
        def send(to, i):
            return remote(hs.at[to * 8 + i], hr.at[pb * TILES + tile], hsend, hrec.at[pb // 4], to, 8 - lax.rem(to, 2) * 8 + i)

        turns = [lax.rem(mine + di, 8) for di in range(8)]
        for start, stop, sites in BLOCKS:
            for p in range(0, 16, 2):
                rhs = jnp.concatenate([cmat[p], cmat[p + 1]], axis=1)
                both = jnp.dot(f[start:stop], rhs, preferred_element_type=F32)
                plain[p, start:stop] = both[:, 0:128]
                plain[p + 1, start:stop] = both[:, 128:256]
            for to in range(start // 8, stop // 8):
                hs[8 * to : 8 * to + 8] = jnp.transpose(plain[:, 8 * to : 8 * to + 8, :], (1, 0, 2)).astype(BF16)
            for there in sites:
                for to in (2 * there, 2 * there + 1):

                    if start == 0:
                        for i in turns:
                            send(to, i).start()
                        continue

                    def one(di, carry):
                        send(to, lax.rem(mine + di, 8)).start()
                        return carry

                    lax.fori_loop(0, 8, one, 0)

    @pl.when(active)
    def _():
        sources = [pairs[1, j] for j in range(16)]
        targets = [kpq[pairs[0, j], sources[j]] for j in range(16)]
        summed = [split_rows(bras, mine, k) for k in range(4)]
        for k in range(4):
            current[k] = as_rows(summed[k])

        def arrived(group):
            some = hr.at[pl.ds(group * 4 * TILES, 4 * TILES)]
            return remote(some, some, hsend, hrec.at[group], sibling, pb)

        for n in range(1, ORDER + 1):
            acc = [jnp.zeros((8, 256), F32) for _ in range(4)]
            for j in range(16):
                if n == 1 and j % 4 == 0:
                    arrived(j // 4).wait_recv()
                if n == 1:
                    unpack(hr, right, j)
                matrix = jnp.concatenate([hr[j * TILES : j * TILES + 8].reshape(128, 128), right[j]], axis=1)
                product = jnp.dot(current[sources[j]], matrix, preferred_element_type=F32)[0:8]
                acc = [acc[k] + jnp.where(targets[j] == k, product, 0.0) for k in range(4)]
            for k in range(4):
                scaled = jnp.concatenate(complex_join(acc[k]), axis=0) * (1.0 / n)
                summed[k] = summed[k] + scaled
                current[k] = as_rows(scaled)
        joined = [
            complex_join(jnp.dot(as_rows(summed[k]), propagator[k], preferred_element_type=F32)) for k in range(4)
        ]
        real, imag = (jnp.concatenate([one[i] for one in joined], axis=0) for i in (0, 1))
        zero = jnp.zeros((16, 128), F32)
        wide = jnp.concatenate([real, zero], axis=1)
        wide += pltpu.roll(jnp.concatenate([imag, zero], axis=1), NORB, 1)
        obuf[mine] = wide.astype(BF16)
        for i in range(1, 16):
            remote(obuf.at[mine], obuf.at[mine], osend, orec, walk, lax.rem(pb + i, 16)).start()
        remote(obuf.at[0:7], obuf.at[0:7], osend, orec, sibling, pb).wait_recv()

    @pl.when(jnp.logical_not(active))
    def _():
        remote(obuf, obuf, osend, orec, sibling, pb).wait_recv()

    for w in range(8):
        rows = obuf[w].astype(F32)
        for k in range(4):
            out[w, k] = rows[4 * k : 4 * k + 4, 0 : 2 * NORB].astype(BF16)

    @pl.when(maker)
    def _():
        remote(packed.at[0:10], packed.at[0:10], csend, crec.at[0], sibling, pb).wait_send()

        remote(hs, hs, hsend, hrec.at[0], sibling, pb).wait_send()

    @pl.when(jnp.logical_not(maker))
    def _():
        remote(packed, packed, csend, crec.at[0], sibling, pb).wait_send()

    @pl.when(active)
    def _():
        remote(hs.at[0:30], hs.at[0:30], osend, orec, sibling, pb).wait_send()


def shards(bras, fields, chol, one_body, pair_table, kpq_map):
    dma = pltpu.SemaphoreType.DMA(())
    return pl.pallas_call(
        kernel,
        out_shape=pltpu.VMEM(bras.shape, BF16),
        in_specs=[pl.BlockSpec(memory_space=pltpu.HBM)] * 6,
        out_specs=pl.BlockSpec(memory_space=pltpu.VMEM),
        scratch_shapes=[
            pltpu.VMEM(bras.shape, BF16),
            pltpu.VMEM(fields.shape, F32),
            pltpu.VMEM(chol.shape, BF16),
            pltpu.VMEM(one_body.shape, BF16),
            pltpu.SMEM((2, 16), jnp.int32),
            pltpu.SMEM((4, 4), jnp.int32),
            pltpu.VMEM((PER, 112, 256), F32),
            pltpu.VMEM((4, 112, 256), F32),
            pltpu.VMEM((4, 128, 256), BF16),
            pltpu.VMEM((TILES, PER + 1, 16, 128), BF16),
            pltpu.VMEM((32, PER + 1, 16, 128), BF16),
            pltpu.VMEM((16, 160, 128), BF16),
            pltpu.VMEM((16, 256, 128), F32),
            pltpu.VMEM((256, 16, 128), BF16),
            pltpu.VMEM((16 * TILES, 16, 128), BF16),
            pltpu.VMEM((16, 128, 128), BF16),
            pltpu.VMEM((4, 16, 128), BF16),
            pltpu.VMEM((8, 16, 256), BF16),
            pltpu.SemaphoreType.DMA((6,)),
            pltpu.SemaphoreType.DMA((4,)),
            dma,
            pltpu.SemaphoreType.DMA((2,)),
            *[dma] * 3,
            pltpu.SemaphoreType.REGULAR,
        ],
        compiler_params=pltpu.CompilerParams(
            collective_id=0, has_side_effects=True, vmem_limit_bytes=60 * 2**20
        ),
        cost_estimate=pl.CostEstimate(flops=10**8, bytes_accessed=10**6, transcendentals=0),
    )(bras, fields, chol, one_body, pair_table.T, kpq_map)


def solution(mesh):
    return jax.shard_map(
        shards,
        mesh=mesh,
        in_specs=(
            P("walk", None, None, None),
            P(None, "walk", None, None),
            P("pb", "walk", None),
            P(),
            P(),
            P(),
        ),
        out_specs=P("walk", None, None, None),
        check_vma=False,
    )
```
